32 devices in a mesh: dp: 8 (over z, core), tensor: 4 (over y, x).
Axes of the slice: x: 2, y: 2, z: 4, core: 2. Of those that a mesh axis runs over, the one named last changes fastest.
Arguments:
- tokens: bfloat16 [12288, 1536], P(('dp', 'tensor')), may hold values from -6 to 6
- cotangent: bfloat16 [12288, 1536], P(('dp', 'tensor')), may hold values from -6 to 6
- lengths: int32 [8, 3], P('dp'), may hold values from 1 to 1024, 1536 in all within a row
- w_qkv: float32 [1536, 2560], P('dp', 'tensor'), may hold values from -0.15625 to 0.15625
- m_qkv: float32 [1536, 2560], P('dp', 'tensor'), may hold values from -64 to 64
- v_qkv: float32 [1536, 2560], P('dp', 'tensor'), may hold values from 651.264 to 2580.48
- w_out: float32 [1536, 1536], P('tensor', 'dp'), may hold values from -0.625 to 0.625
- m_out: float32 [1536, 1536], P('tensor', 'dp'), may hold values from -20 to 20
- v_out: float32 [1536, 1536], P('tensor', 'dp'), may hold values from 58.9824 to 233.472
- w_gateup: float32 [2, 1536, 6912], P(None, 'dp', 'tensor'), may hold values from -0.15625 to 0.15625
- m_gateup: float32 [2, 1536, 6912], P(None, 'dp', 'tensor'), may hold values from -20 to 20
- v_gateup: float32 [2, 1536, 6912], P(None, 'dp', 'tensor'), may hold values from 58.9824 to 233.472
- w_down: float32 [6912, 1536], P('tensor', 'dp'), may hold values from -0.078125 to 0.078125
- m_down: float32 [6912, 1536], P('tensor', 'dp'), may hold values from -40 to 40
- v_down: float32 [6912, 1536], P('tensor', 'dp'), may hold values from 233.472 to 933.888
- gains: float32 [3200], replicated, may hold values from 0.5 to 1.5
- m_gains: float32 [3200], replicated, may hold values from -64 to 64
- v_gains: float32 [3200], replicated, may hold values from 651.264 to 2580.48
Outputs:
- output: bfloat16 [12288, 1536], P(('dp', 'tensor'))
- grad_tokens: float32 [12288, 1536], P(('dp', 'tensor'))
- new_w_qkv: float32 [1536, 2560], P('dp', 'tensor')
- new_m_qkv: float32 [1536, 2560], P('dp', 'tensor')
- new_v_qkv: float32 [1536, 2560], P('dp', 'tensor')
- new_w_out: float32 [1536, 1536], P('tensor', 'dp')
- new_m_out: float32 [1536, 1536], P('tensor', 'dp')
- new_v_out: float32 [1536, 1536], P('tensor', 'dp')
- new_w_gateup: float32 [2, 1536, 6912], P(None, 'dp', 'tensor')
- new_m_gateup: float32 [2, 1536, 6912], P(None, 'dp', 'tensor')
- new_v_gateup: float32 [2, 1536, 6912], P(None, 'dp', 'tensor')
- new_w_down: float32 [6912, 1536], P('tensor', 'dp')
- new_m_down: float32 [6912, 1536], P('tensor', 'dp')
- new_v_down: float32 [6912, 1536], P('tensor', 'dp')
- new_gains: float32 [3200], replicated
- new_m_gains: float32 [3200], replicated
- new_v_gains: float32 [3200], replicated
The draws below stay inside these ranges and needn't reach their ends.
Inputs may be any that keep to these rules, and one draw needn't show every extreme that they name: Row r holds, in order, the lengths of the sequences packed on the 1536 tokens of index r of dp; each row sums to 1536 and its longest is 1024.
All inputs are finite; a program needn't handle non-finite values.
Results may differ from the reference program's by a relative error of at most 0.024.
Values may be sent and summed in bfloat16 or wider, within the bound.
No kernel may reach another device: no remote copies, remote signals or barrier semaphores. Data moves between devices by JAX's collectives and lax.ppermute only.
A program may use at most 256 MiB of HBM per device.

```python
import math
import jax
import jax.numpy as jnp
import numpy as np
from jax import lax

D = 1536
HEADS = 24
KV = 8
HD = 64
FF = 6912
TOK_DEV = 1536
MAXLEN = 1024
STEP = 10
SEQS = 3
QKV = 2560
TOKENS = 12288
GAINS = 3200
N_DP = 8


def shard_levels(own_key, extent, split, least, largest):
    factor_of, own = 1.0, jax.random.fold_in(own_key, 6)
    for dim, blocks in split:
        draws = jnp.exp(jax.random.uniform(jax.random.fold_in(own, dim), (blocks,), jnp.float32, least / len(split), largest / len(split)))
        factor_of = factor_of * jnp.repeat(draws, extent[dim] // blocks).reshape([-1 if axis == dim else 1 for axis in range(len(extent))])
    return factor_of


def split_up(count, total, reach, skew):
    loads = [(1 << 20) // math.isqrt(grade ** skew) + 1 for grade in range(2, count + 1)]
    spare, holding = total - reach - (count - 1), [1] * (count - 1)
    while spare > 0:
        movable = [i for i in range(count - 1) if holding[i] < reach]
        whole, budget = sum([loads[i] for i in movable]), spare
        for i in movable:
            extra = min(reach - holding[i], max(1, budget * loads[i] // whole), spare)
            holding[i] = holding[i] + extra
            spare = spare - extra
    return np.array([reach] + holding)


def ragged(rng, amount, total, bound, skew):
    if amount == 2:
        one = jax.random.randint(rng, (), max(1, total - bound), min(bound, total - 1) + 1)
        return jnp.stack([one, total - one])
    tallies = jnp.asarray(split_up(amount, total, bound, skew), jnp.int32)
    twos = (amount - 1) // 2
    source_of, receiver = tallies[1:1 + 2 * twos:2], tallies[2:2 + 2 * twos:2]
    slack = jnp.minimum(source_of - 1, bound - receiver)
    shifted = jax.random.randint(jax.random.fold_in(rng, 1), (twos,), 0, 1 << 20) % (slack + 1)
    tallies = tallies.at[1:1 + 2 * twos:2].set(source_of - shifted).at[2:2 + 2 * twos:2].set(receiver + shifted)
    return tallies[jax.random.permutation(jax.random.fold_in(rng, 2), amount)]


def scatter_about(stream_key, extent, spread, most, cuts=(), kind=jnp.bfloat16):
    values = jax.random.normal(stream_key, extent, jnp.float32) * spread
    if len(cuts) > 0:
        values = shard_levels(stream_key, extent, cuts, -0.22, 0.18) * values
    return jnp.clip(values, min=-most, max=most).astype(kind)


def setup_inputs(seed: int = 0) -> dict:
    key_of = jax.random.split(jax.random.key(seed), 19)
    return {
        "tokens": scatter_about(key_of[0], (TOKENS, D), 1.0, 6.0, ((0, 32),)),
        "cotangent": scatter_about(key_of[1], (TOKENS, D), 1.0, 6.0, ((0, 32),)),
        "lengths": jax.vmap(lambda own: ragged(own, SEQS, TOK_DEV, MAXLEN, 2))(jax.random.split(key_of[2], N_DP)).reshape((N_DP, SEQS)).astype(jnp.int32),
        "w_qkv": scatter_about(key_of[3], (D, QKV), D ** -0.5, 0.15625, ((0, 8), (1, 4)), jnp.float32),
        "m_qkv": scatter_about(key_of[4], (D, QKV), (0.11 * TOKENS ** 0.5), 64.0, ((0, 8), (1, 4)), jnp.float32),
        "v_qkv": jnp.clip(jnp.exp(math.log(2580.48) - 1.37681564 * jax.random.uniform(key_of[5], (D, QKV), jnp.float32) ** shard_levels(key_of[5], (D, QKV), ((0, 8), (1, 4)), -0.2, 0.2)), 651.264, 2580.48),
        "w_out": scatter_about(key_of[6], (HEADS * HD, D), (HEADS * HD // 16) ** -0.5, 0.625, ((0, 4), (1, 8)), jnp.float32),
        "m_out": scatter_about(key_of[7], (HEADS * HD, D), (0.033 * TOKENS ** 0.5), 20.0, ((0, 4), (1, 8)), jnp.float32),
        "v_out": jnp.clip(jnp.exp(math.log(233.472) - 1.375823 * jax.random.uniform(key_of[8], (HEADS * HD, D), jnp.float32) ** shard_levels(key_of[8], (HEADS * HD, D), ((0, 4), (1, 8)), -0.2, 0.2)), 58.9824, 233.472),
        "w_gateup": scatter_about(key_of[9], (2, D, FF), D ** -0.5, 0.15625, ((1, 8), (2, 4)), jnp.float32),
        "m_gateup": scatter_about(key_of[10], (2, D, FF), (0.033 * TOKENS ** 0.5), 20.0, ((1, 8), (2, 4)), jnp.float32),
        "v_gateup": jnp.clip(jnp.exp(math.log(233.472) - 1.375823 * jax.random.uniform(key_of[11], (2, D, FF), jnp.float32) ** shard_levels(key_of[11], (2, D, FF), ((1, 8), (2, 4)), -0.2, 0.2)), 58.9824, 233.472),
        "w_down": scatter_about(key_of[12], (FF, D), FF ** -0.5, 0.078125, ((0, 4), (1, 8)), jnp.float32),
        "m_down": scatter_about(key_of[13], (FF, D), (0.066 * TOKENS ** 0.5), 40.0, ((0, 4), (1, 8)), jnp.float32),
        "v_down": jnp.clip(jnp.exp(math.log(933.888) - 1.3862944 * jax.random.uniform(key_of[14], (FF, D), jnp.float32) ** shard_levels(key_of[14], (FF, D), ((0, 4), (1, 8)), -0.2, 0.2)), 233.472, 933.888),
        "gains": jnp.clip(1.0 + 0.1 * jax.random.normal(key_of[15], (GAINS,), jnp.float32), 0.5, 1.5),
        "m_gains": scatter_about(key_of[16], (GAINS,), (0.11 * TOKENS ** 0.5), 64.0, (), jnp.float32),
        "v_gains": jnp.clip(jnp.exp(jax.random.uniform(key_of[17], (GAINS,), jnp.float32, math.log(651.264), math.log(2580.48))), 651.264, 2580.48),
    }


NORM_EPS = 1e-05
ROPE_BASE = 1000000.0
BETA_ONE = 0.9
BETA_TWO = 0.95
ADAM_EPS = 1e-08
WEIGHT_DECAY = 0.1
MATRIX_RATE = 0.05
GAIN_RATE = 0.5
MASKED = -1e+30
PRECISE = lax.Precision.HIGHEST

@jax.custom_vjp
def low(v):
    return lax.optimization_barrier(v.astype(jnp.bfloat16)).astype(jnp.float32)

@jax.custom_vjp
def low_back(v):
    return v

def low_keep(v):
    return (low(v), None)

def low_pass(kept, grad):
    return (grad,)

def back_keep(v):
    return (v, None)

def back_low(kept, grad):
    return (low(grad),)
low.defvjp(low_keep, low_pass)
low_back.defvjp(back_keep, back_low)

def rms_norm(values, gain):
    return values * lax.rsqrt(lax.optimization_barrier(jnp.mean(values * values, axis=-1, keepdims=True)) + NORM_EPS) * gain

def rotate(values, cosine, sine_part):
    half_width = values.shape[-1] // 2
    first_half = values[..., :half_width]
    second_half = values[..., half_width:]
    return jnp.concatenate([first_half * cosine - second_half * sine_part, second_half * cosine + first_half * sine_part], axis=-1)

def layout(counts, row_count):
    ends_at = jnp.cumsum(counts).astype(jnp.int32)
    starts = (ends_at - counts).astype(jnp.int32)
    place_idx = jnp.arange(row_count, dtype=jnp.int32)
    owners = lax.optimization_barrier(jnp.sum((place_idx[:, None] >= ends_at[None, :]).astype(jnp.int32), axis=1)).astype(jnp.int32)
    slots = jnp.arange(counts.shape[0], dtype=jnp.int32)
    begin_at = lax.optimization_barrier(jnp.sum(jnp.where(owners[:, None] == slots[None, :], starts[None, :], 0), axis=1)).astype(jnp.int32)
    return (owners, (place_idx - begin_at).astype(jnp.int32))

def angles(positions, head_width):
    half_width = head_width // 2
    frequency = ROPE_BASE ** (-(jnp.arange(half_width, dtype=jnp.float32) * 2.0 / head_width))
    turn_angle = positions.astype(jnp.float32)[:, None] * frequency[None, :]
    return (jnp.cos(turn_angle), jnp.sin(turn_angle))

def block_attend(queries, keys_all, values, owners):
    row_count = queries.shape[0]
    scores = jnp.einsum('qgjd,kgd->gjqk', queries, keys_all, precision=PRECISE) * HD ** (-0.5)
    scores = low_back(scores)
    place_idx = jnp.arange(row_count, dtype=jnp.int32)
    admitted = (owners[:, None] == owners[None, :]) & (place_idx[None, :] <= place_idx[:, None])
    scores = jnp.where(admitted, scores, MASKED)
    maximum = lax.optimization_barrier(jnp.max(scores, axis=-1, keepdims=True))
    exponent = jnp.exp(scores - maximum)
    probs_full = low(exponent / lax.optimization_barrier(jnp.sum(exponent, axis=-1, keepdims=True)))
    return jnp.einsum('gjqk,kgd->qgjd', probs_full, values, precision=PRECISE)

def attend_one(pieces):
    return block_attend(pieces[0], pieces[1], pieces[2], pieces[3])

def forward(inputs, weight_qkv, weight_out, weight_gateup, weight_down, gain_all, owners, positions):
    row_count = inputs.shape[0]
    per_group = HEADS // KV
    gain_attn = gain_all[:D]
    gain_ffn = gain_all[D:2 * D]
    gain_query = gain_all[2 * D:2 * D + HD]
    gain_key = gain_all[2 * D + HD:]
    normed = low(rms_norm(inputs, gain_attn))
    mixed_qkv = low_back(jnp.dot(normed, weight_qkv, precision=PRECISE)).reshape(row_count, KV, per_group + 2, HD)
    cosine, sine_part = angles(positions, HD)
    queries = low(rotate(rms_norm(mixed_qkv[:, :, :per_group], gain_query), cosine[:, None, None], sine_part[:, None, None]))
    keys_all = low(rotate(rms_norm(mixed_qkv[:, :, per_group], gain_key), cosine[:, None], sine_part[:, None]))
    values = low(mixed_qkv[:, :, per_group + 1])
    attended = lax.map(jax.checkpoint(attend_one), (queries.reshape(N_DP, TOK_DEV, KV, per_group, HD), keys_all.reshape(N_DP, TOK_DEV, KV, HD), values.reshape(N_DP, TOK_DEV, KV, HD), owners.reshape(N_DP, TOK_DEV)))
    attended = low(low_back(attended.reshape(row_count, HEADS * HD)))
    branch = low_back(jnp.dot(attended, weight_out, precision=PRECISE))
    middle = inputs + branch
    second = low(rms_norm(middle, gain_ffn))
    gate_pre = low_back(jnp.dot(second, weight_gateup[0], precision=PRECISE))
    upward = low_back(jnp.dot(second, weight_gateup[1], precision=PRECISE))
    hidden = low(jax.nn.silu(gate_pre) * upward)
    return middle + jnp.dot(hidden, weight_down, precision=PRECISE)

def adamw_step(weight, first_old, second_old, gradient, step_rate):
    first_new = BETA_ONE * first_old + (1.0 - BETA_ONE) * gradient
    second_new = BETA_TWO * second_old + (1.0 - BETA_TWO) * gradient * gradient
    first_fixed = first_new / (1.0 - BETA_ONE ** STEP)
    second_fixed = second_new / (1.0 - BETA_TWO ** STEP)
    weight_new = weight - step_rate * (first_fixed / (jnp.sqrt(second_fixed) + ADAM_EPS) + WEIGHT_DECAY * weight)
    return (weight_new, first_new, second_new)

def reference(tokens, cotangent, lengths, w_qkv, m_qkv, v_qkv, w_out, m_out, v_out, w_gateup, m_gateup, v_gateup, w_down, m_down, v_down, gains, m_gains, v_gains):
    owners, positions = jax.vmap(lambda counts: layout(counts, TOK_DEV))(lengths)
    owners = owners.reshape(-1)
    positions = positions.reshape(-1)

    def closed(inputs, weight_qkv, weight_out, weight_gateup, weight_down, gain_all):
        return forward(inputs, weight_qkv, weight_out, weight_gateup, weight_down, gain_all, owners, positions)
    result, pullback = jax.vjp(closed, tokens.astype(jnp.float32), low(w_qkv), low(w_out), low(w_gateup), low(w_down), gains)
    grads = pullback(cotangent.astype(jnp.float32))
    qkv_new = adamw_step(w_qkv, m_qkv, v_qkv, grads[1], MATRIX_RATE)
    out_new = adamw_step(w_out, m_out, v_out, grads[2], MATRIX_RATE)
    gateup_new = adamw_step(w_gateup, m_gateup, v_gateup, grads[3], MATRIX_RATE)
    down_new = adamw_step(w_down, m_down, v_down, grads[4], MATRIX_RATE)
    gains_new = adamw_step(gains, m_gains, v_gains, grads[5], GAIN_RATE)
    return (result.astype(jnp.bfloat16), grads[0], qkv_new[0], qkv_new[1], qkv_new[2], out_new[0], out_new[1], out_new[2], gateup_new[0], gateup_new[1], gateup_new[2], down_new[0], down_new[1], down_new[2], gains_new[0], gains_new[1], gains_new[2])
```

```python
import functools
import math

import jax
import jax.numpy as jnp
from jax import lax
from jax.experimental import pallas as pl
from jax.experimental.pallas import tpu as pltpu
from jax.sharding import PartitionSpec as P

HEADS = 24
KV = 8
HD = 64
STEP = 10
PER = HEADS // KV

NORM_EPS = 1e-05
ROPE_BASE = 1000000.0
BETA_ONE = 0.9
BETA_TWO = 0.95
ADAM_EPS = 1e-08
WEIGHT_DECAY = 0.1
MATRIX_RATE = 0.05
GAIN_RATE = 0.5

LANES = 128
BLK = 256
LOG2E = math.log2(math.e)
VMEM_LIMIT = 48 * 1024 * 1024
BF16 = jnp.bfloat16
F32 = jnp.float32
NN = (((1,), (0,)), ((), ()))
NT = (((1,), (1,)), ((), ()))
TN = (((0,), (0,)), ((), ()))


def mm(left, right, dims=NN):
    return lax.dot_general(left, right, dims, preferred_element_type=F32)


def norm_rows(values, gain):
    return values * lax.rsqrt(jnp.mean(values * values, axis=-1, keepdims=True) + NORM_EPS) * gain


def layout(counts, row_count):
    ends_at = jnp.cumsum(counts)
    starts = ends_at - counts
    place_idx = jnp.arange(row_count, dtype=jnp.int32)
    owners = jnp.sum((place_idx[:, None] >= ends_at[None, :]).astype(jnp.int32), axis=1)
    slots = jnp.arange(counts.shape[0], dtype=jnp.int32)
    begin_at = jnp.sum(jnp.where(owners[:, None] == slots[None, :], starts[None, :], 0), axis=1)
    return begin_at, place_idx - begin_at


def angles(positions):
    half_width = HD // 2
    frequency = ROPE_BASE ** (-(jnp.arange(half_width, dtype=F32) * 2.0 / HD))
    turn_angle = positions.astype(F32)[:, None] * frequency[None, :]
    return (jnp.cos(turn_angle), jnp.sin(turn_angle))


def adamw_step(weight, first_old, second_old, gradient, step_rate):
    first_new = BETA_ONE * first_old + (1.0 - BETA_ONE) * gradient
    second_new = BETA_TWO * second_old + (1.0 - BETA_TWO) * gradient * gradient
    first_fixed = first_new / (1.0 - BETA_ONE**STEP)
    second_fixed = second_new / (1.0 - BETA_TWO**STEP)
    weight_new = weight - step_rate * (
        first_fixed / (jnp.sqrt(second_fixed) + ADAM_EPS) + WEIGHT_DECAY * weight
    )
    return (weight_new, first_new, second_new)


def piece_places(count, chunk):
    places = [(j, 0, chunk) for j in (0, 1, 2) if j < count]
    bit = len(places)
    if count >= 4:
        half = chunk // 2
        places += [(3, 0, half), (3, half, half)]
        bit = 4
    while bit < count:
        places += [(j | bit, off, rows) for j, off, rows in places]
        bit *= 2
    return places


def gather_copies(piece_refs, dst_ref, sems, mine, count):
    chunk = dst_ref.shape[0] // count
    copies = []
    for idx, (slot, off, rows) in enumerate(piece_places(count, chunk)):
        row = pl.multiple_of(jnp.bitwise_xor(mine, slot) * chunk + off, chunk // 2)
        copies.append(
            pltpu.make_async_copy(
                piece_refs[idx], dst_ref.at[pl.ds(row, rows), :], sems.at[idx]
            )
        )
    return copies


def gather_pieces(piece_refs, dst_ref, sems, mine, count):
    copies = gather_copies(piece_refs, dst_ref, sems, mine, count)
    for copy in copies:
        copy.start()
    for copy in copies:
        copy.wait()


def half_sums(values):
    row = lax.broadcasted_iota(jnp.int32, (LANES, LANES), 0) // HD
    col = lax.broadcasted_iota(jnp.int32, (LANES, LANES), 1) // HD
    ones = jnp.where(row == col, 1.0, 0.0).astype(BF16)
    high = values.astype(BF16)
    rest = (values - high.astype(F32)).astype(BF16)
    return mm(high, ones) + mm(rest, ones)


def swap_halves(values):
    lane = lax.broadcasted_iota(jnp.int32, values.shape, 1)
    half = HD // 2
    return jnp.where(
        (lane % HD) < half, pltpu.roll(values, LANES - half, 1), pltpu.roll(values, half, 1)
    )


def split_two(values):
    high = values.astype(BF16).astype(F32)
    return high, values - high


def low_lanes(rows):
    return lax.broadcasted_iota(jnp.int32, (rows, LANES), 1) < HD


def fwd_kernel(heads, groups, count, scalars, *refs):
    places = len(piece_places(count, 2))
    pieces, refs = refs[:places], refs[places:]
    w_ref, cos_ref, sin_ref, gains_ref, start_ref = refs[:5]
    out_ref, mixed_ref, rows_ref, qaug_ref, kaug_ref, vaug_ref = refs[5:11]
    x_ref, vt_ref, acc_ref, sems, rows_sem = refs[11:]
    rows = x_ref.shape[0]
    q_tiles = (heads + 1) // 2
    k_tiles = (groups + 1) // 2
    qkv_width = mixed_ref.shape[1]
    gather_pieces(pieces, x_ref, sems, scalars[rows // BLK], count)
    keep_rows = pltpu.make_async_copy(x_ref, rows_ref, rows_sem)
    keep_rows.start()

    def prep(blk, _):
        at = pl.ds(pl.multiple_of(blk * BLK, BLK), BLK)
        cos = cos_ref[at, :]
        sin = sin_ref[at, :]
        lane = lax.broadcasted_iota(jnp.int32, (BLK, LANES), 1)
        low = lane < HD
        mixed = mm(x_ref[at, :], w_ref[:, :qkv_width])
        mixed_ref[at, :] = mixed

        def turned(tile, which):
            raw = mixed[:, tile * LANES : (tile + 1) * LANES]
            scaled = raw * lax.rsqrt(half_sums(raw * raw) * (1.0 / HD) + NORM_EPS)
            scaled = scaled * gains_ref[which : which + 1, :]
            return scaled * cos + swap_halves(scaled) * sin

        for tile in range(q_tiles):
            query = turned(tile, 0) * (LOG2E * HD**-0.5)
            qaug_ref[2 * tile, at, :] = jnp.where(low, query, 0.0).astype(BF16)
            if 2 * tile + 1 < heads:
                other = jnp.where(low, pltpu.roll(query, HD, 1), 0.0)
                qaug_ref[2 * tile + 1, at, :] = other.astype(BF16)
        ones = jnp.where((lane == HD) | (lane == HD + 1), 1.0, 0.0)
        for tile in range(k_tiles):
            key = turned(q_tiles + tile, 1)
            v_at = (q_tiles + k_tiles + tile) * LANES
            value = mixed[:, v_at : v_at + LANES]
            for side in range(min(2, groups - 2 * tile)):
                if side:
                    key = pltpu.roll(key, HD, 1)
                    value = pltpu.roll(value, HD, 1)
                own_value = jnp.where(low, value, ones)
                kaug_ref[2 * tile + side, at, :] = jnp.where(low, key, ones).astype(BF16)
                vaug_ref[2 * tile + side, at, :] = own_value.astype(BF16)
                vt_ref[2 * tile + side, :, at] = jnp.transpose(own_value).astype(BF16)
        return 0

    lax.fori_loop(0, rows // BLK, prep, 0)
    key_idx = lax.broadcasted_iota(jnp.int32, (BLK, BLK), 0)
    ahead = key_idx - lax.broadcasted_iota(jnp.int32, (BLK, BLK), 1)

    def per_query(q_blk, _):
        q_at = pl.ds(pl.multiple_of(q_blk * BLK, BLK), BLK)
        acc_ref[...] = jnp.zeros_like(acc_ref)
        start = start_ref[0:1, q_at]

        def per_key(k_blk, _):
            k_at = pl.ds(pl.multiple_of(k_blk * BLK, BLK), BLK)
            admitted = (key_idx >= start - k_blk * BLK) & (ahead <= (q_blk - k_blk) * BLK)
            for group in range(groups):
                query = qaug_ref[group * PER : (group + 1) * PER, q_at, :]
                scores = mm(kaug_ref[group, k_at, :], query.reshape(PER * BLK, LANES), NT)
                probs = [
                    jnp.where(admitted, jnp.exp2(scores[:, j * BLK : (j + 1) * BLK]), 0.0)
                    for j in range(PER)
                ]
                probs = jnp.concatenate([p.astype(BF16) for p in probs], axis=1)
                acc_ref[group] += mm(vt_ref[group, :, k_at], probs)
            return 0

        lax.fori_loop(scalars[q_blk], q_blk + 1, per_key, 0)
        low = low_lanes(BLK)
        kept = None
        for head in range(heads):
            raw = acc_ref[head // PER, :, (head % PER) * BLK : (head % PER + 1) * BLK]
            total = raw[HD : HD + 1, :]
            high, rest = split_two(jnp.log2(total))
            sub = lax.broadcasted_iota(jnp.int32, raw.shape, 0)
            tail = jnp.where(sub == HD, -high, jnp.where(sub == HD + 1, -rest, 0.0))
            whole = jnp.transpose(jnp.where(sub < HD, raw * (1.0 / total), tail))
            query = qaug_ref[head, q_at, :].astype(F32)
            qaug_ref[head, q_at, :] = jnp.where(low, query, whole).astype(BF16)
            if head % 2 == 0:
                kept = whole
            if head % 2 == 1 or head == heads - 1:
                second = pltpu.roll(whole, HD, 1) if head % 2 == 1 else jnp.zeros_like(whole)
                cols = slice(head // 2 * LANES, (head // 2 + 1) * LANES)
                out_ref[q_at, cols] = jnp.where(low, kept, second).astype(BF16)
        return 0

    lax.fori_loop(0, rows // BLK, per_query, 0)
    keep_rows.wait()


def bwd_kernel(heads, groups, count, scalars, *refs):
    places = len(piece_places(count, 2))
    pieces, refs = refs[:places], refs[places:]
    w_ref, mixed_ref, cos_ref, sin_ref, gains_ref, start_ref = refs[:6]
    out_ref, qaug_ref, kaug_ref, vaug_ref = refs[6:10]
    gm_ref, gg_ref, rows_ref = refs[10:13]
    x_ref, daug_ref, kt_ref, dq_ref, dk_ref, dv_ref, sems, rows_sem = refs[13:]
    rows = x_ref.shape[0]
    q_tiles = (heads + 1) // 2
    k_tiles = (groups + 1) // 2
    qkv_width = mixed_ref.shape[1]
    gather_pieces(pieces, x_ref, sems, scalars[rows // BLK], count)
    keep_rows = pltpu.make_async_copy(x_ref, rows_ref, rows_sem)
    keep_rows.start()

    def prep(blk, _):
        at = pl.ds(pl.multiple_of(blk * BLK, BLK), BLK)
        lane = lax.broadcasted_iota(jnp.int32, (BLK, LANES), 1)
        low = lane < HD
        grads = mm(x_ref[at, :], w_ref[:, qkv_width:]).astype(BF16).astype(F32)
        for tile in range(q_tiles):
            grad = grads[:, tile * LANES : (tile + 1) * LANES]
            out = out_ref[at, tile * LANES : (tile + 1) * LANES].astype(F32)
            high, rest = split_two(-half_sums(grad * out))
            tail = jnp.where(lane % HD == 0, high, jnp.where(lane % HD == 1, rest, 0.0))
            daug_ref[2 * tile, at, :] = jnp.where(low, grad, pltpu.roll(tail, HD, 1)).astype(BF16)
            if 2 * tile + 1 < heads:
                other = jnp.where(low, pltpu.roll(grad, HD, 1), tail)
                daug_ref[2 * tile + 1, at, :] = other.astype(BF16)
        for group in range(groups):
            kt_ref[group, :, at] = jnp.transpose(kaug_ref[group, at, :].astype(F32)).astype(BF16)
        return 0

    lax.fori_loop(0, rows // BLK, prep, 0)
    dk_ref[...] = jnp.zeros_like(dk_ref)
    dv_ref[...] = jnp.zeros_like(dv_ref)
    gg_ref[...] = jnp.zeros_like(gg_ref)
    key_idx = lax.broadcasted_iota(jnp.int32, (BLK, BLK), 0)
    ahead = key_idx - lax.broadcasted_iota(jnp.int32, (BLK, BLK), 1)

    def finish(at, tile, which, grad):
        cols = slice(tile * LANES, (tile + 1) * LANES)
        raw = mixed_ref[at, cols]
        back = grad * cos_ref[at, :] - swap_halves(grad) * sin_ref[at, :]
        scale = lax.rsqrt(half_sums(raw * raw) * (1.0 / HD) + NORM_EPS)
        unscaled = raw * scale
        gg_ref[which : which + 1, :] += jnp.sum(back * unscaled, axis=0, keepdims=True)
        back = back * gains_ref[which : which + 1, :]
        mean = half_sums(unscaled * back) * (1.0 / HD)
        gm_ref[at, cols] = (scale * (back - unscaled * mean)).astype(BF16)

    def per_query(q_blk, _):
        q_at = pl.ds(pl.multiple_of(q_blk * BLK, BLK), BLK)
        start = start_ref[0:1, q_at]
        dq_ref[...] = jnp.zeros_like(dq_ref)

        def per_key(k_blk, _):
            k_at = pl.ds(pl.multiple_of(k_blk * BLK, BLK), BLK)
            admitted = (key_idx >= start - k_blk * BLK) & (ahead <= (q_blk - k_blk) * BLK)
            for group in range(groups):
                own = slice(group * PER, (group + 1) * PER)
                query = qaug_ref[own, q_at, :].reshape(PER * BLK, LANES)
                grad = daug_ref[own, q_at, :].reshape(PER * BLK, LANES)
                scores = mm(kaug_ref[group, k_at, :], query, NT)
                grad_probs = mm(vaug_ref[group, k_at, :], grad, NT)
                probs, grad_scores = [], []
                for j in range(PER):
                    cols = slice(j * BLK, (j + 1) * BLK)
                    prob = jnp.where(admitted, jnp.exp2(scores[:, cols]), 0.0)
                    probs.append(prob.astype(BF16))
                    grad_scores.append((prob * grad_probs[:, cols]).astype(BF16))
                probs = jnp.concatenate(probs, axis=1)
                grad_scores = jnp.concatenate(grad_scores, axis=1)
                dv_ref[group, k_at, :] += mm(probs, grad)
                dk_ref[group, k_at, :] += mm(grad_scores, query)
                dq_ref[group] += mm(kt_ref[group, :, k_at], grad_scores)
            return 0

        lax.fori_loop(scalars[q_blk], q_blk + 1, per_key, 0)
        low = low_lanes(BLK)
        for tile in range(q_tiles):
            pair = []
            for head in range(2 * tile, 2 * tile + 2):
                if head < heads:
                    cols = slice((head % PER) * BLK, (head % PER + 1) * BLK)
                    own = jnp.transpose(dq_ref[head // PER, :, cols])
                    pair.append(pltpu.roll(own, HD, 1) if head % 2 else own)
                else:
                    pair.append(jnp.zeros((BLK, LANES), F32))
            finish(q_at, tile, 0, jnp.where(low, pair[0], pair[1]) * HD**-0.5)
        return 0

    lax.fori_loop(0, rows // BLK, per_query, 0)

    def per_key_block(blk, _):
        at = pl.ds(pl.multiple_of(blk * BLK, BLK), BLK)
        low = low_lanes(BLK)

        def joined(ref, tile):
            first = ref[2 * tile, at, :]
            if 2 * tile + 1 < groups:
                return jnp.where(low, first, pltpu.roll(ref[2 * tile + 1, at, :], HD, 1))
            return jnp.where(low, first, 0.0)

        for tile in range(k_tiles):
            finish(at, q_tiles + tile, 1, joined(dk_ref, tile) * (1.0 / LOG2E))
            v_at = (q_tiles + k_tiles + tile) * LANES
            gm_ref[at, v_at : v_at + LANES] = joined(dv_ref, tile).astype(BF16)
        return 0

    lax.fori_loop(0, rows // BLK, per_key_block, 0)
    keep_rows.wait()


IN_VMEM = pl.BlockSpec(memory_space=pltpu.VMEM)
IN_SMEM = pl.BlockSpec(memory_space=pltpu.SMEM)
IN_ANY = pl.BlockSpec(memory_space=pl.ANY)
PARAMS = pltpu.CompilerParams(vmem_limit_bytes=VMEM_LIMIT)


def like(*shape, dtype=BF16):
    return jax.ShapeDtypeStruct(shape, dtype)


def cost(flops, moved, special=0):
    return pl.CostEstimate(flops=flops, bytes_accessed=moved, transcendentals=special)


def attend(scalars, pieces, full_attn, tables, heads, groups, count):
    width = pieces[0].shape[1]
    rows = pieces[0].shape[0] * count
    q_tiles, k_tiles = (heads + 1) // 2, (groups + 1) // 2
    qkv_width = (q_tiles + 2 * k_tiles) * LANES
    pairs = heads * rows * rows
    return pl.pallas_call(
        functools.partial(fwd_kernel, heads, groups, count),
        out_shape=(
            like(rows, q_tiles * LANES),
            like(rows, qkv_width, dtype=F32),
            like(rows, width),
            like(heads, rows, LANES),
            like(groups, rows, LANES),
            like(groups, rows, LANES),
        ),
        in_specs=[IN_SMEM] + [IN_ANY] * len(pieces) + [IN_VMEM] * 5,
        out_specs=(IN_VMEM, IN_VMEM, IN_ANY, IN_VMEM, IN_VMEM, IN_VMEM),
        scratch_shapes=[
            pltpu.VMEM((rows, width), BF16),
            pltpu.VMEM((groups, LANES, rows), BF16),
            pltpu.VMEM((groups, LANES, PER * BLK), F32),
            pltpu.SemaphoreType.DMA((len(pieces),)),
            pltpu.SemaphoreType.DMA,
        ],
        compiler_params=PARAMS,
        cost_estimate=cost(8 * pairs * LANES, 8 * rows * width, pairs),
        name="attend",
    )(scalars, *pieces, full_attn, *tables)


def attend_back(scalars, pieces, full_attn, mixed, tables, saved, heads, groups, count):
    width = pieces[0].shape[1]
    rows = pieces[0].shape[0] * count
    pairs = heads * rows * rows
    return pl.pallas_call(
        functools.partial(bwd_kernel, heads, groups, count),
        out_shape=(like(*mixed.shape), like(8, LANES, dtype=F32), like(rows, width)),
        in_specs=[IN_SMEM] + [IN_ANY] * len(pieces) + [IN_VMEM] * 10,
        out_specs=(IN_VMEM, IN_VMEM, IN_ANY),
        scratch_shapes=[
            pltpu.VMEM((rows, width), BF16),
            pltpu.VMEM((heads, rows, LANES), BF16),
            pltpu.VMEM((groups, LANES, rows), BF16),
            pltpu.VMEM((groups, LANES, PER * BLK), F32),
            pltpu.VMEM((groups, rows, LANES), F32),
            pltpu.VMEM((groups, rows, LANES), F32),
            pltpu.SemaphoreType.DMA((len(pieces),)),
            pltpu.SemaphoreType.DMA,
        ],
        compiler_params=PARAMS,
        cost_estimate=cost(12 * pairs * LANES, 8 * rows * width, pairs),
        name="attend_back",
    )(scalars, *pieces, full_attn, mixed, *tables, *saved)


def gateup_kernel(count, mine_ref, *refs):
    places = len(piece_places(count, 2))
    pieces, refs = refs[:places], refs[places:]
    w_ref, hidden_ref, gate_ref, up_ref, rows_ref, x_ref, sems, rows_sem = refs
    keep_rows = pltpu.make_async_copy(x_ref, rows_ref, rows_sem)
    step = pl.program_id(0)

    @pl.when(step == 0)
    def _():
        gather_pieces(pieces, x_ref, sems, mine_ref[0], count)
        keep_rows.start()

    w_gate = w_ref[0]
    w_up = w_ref[1]
    for row in range(0, x_ref.shape[0], BLK):
        at = slice(row, row + BLK)
        gate = mm(x_ref[at, :], w_gate)
        up = mm(x_ref[at, :], w_up)
        sigmoid = jax.nn.sigmoid(gate)
        silu = gate * sigmoid
        hidden_ref[at, :] = (silu * up).astype(BF16)
        gate_ref[at, :] = (up * sigmoid * (1.0 + (gate - silu))).astype(BF16)
        up_ref[at, :] = silu.astype(BF16)

    @pl.when(step == pl.num_programs(0) - 1)
    def _():
        keep_rows.wait()


def gateup_forward(mine, pieces, full_gateup, count):
    width = pieces[0].shape[1]
    rows = pieces[0].shape[0] * count
    units = full_gateup.shape[2]
    tile = pl.BlockSpec((rows, BLK), lambda i: (0, i))
    return pl.pallas_call(
        functools.partial(gateup_kernel, count),
        grid=(pl.cdiv(units, BLK),),
        out_shape=(like(rows, units),) * 3 + (like(rows, width),),
        in_specs=[IN_SMEM]
        + [IN_ANY] * len(pieces)
        + [pl.BlockSpec((2, width, BLK), lambda i: (0, 0, i))],
        out_specs=(tile, tile, tile, IN_ANY),
        scratch_shapes=[
            pltpu.VMEM((rows, width), BF16),
            pltpu.SemaphoreType.DMA((len(pieces),)),
            pltpu.SemaphoreType.DMA,
        ],
        compiler_params=PARAMS,
        cost_estimate=cost(4 * rows * width * units, 2 * units * (2 * width + 3 * rows)),
        name="gateup",
    )(mine, *pieces, full_gateup)


def down_grad_kernel(count, mine_ref, *refs):
    places = len(piece_places(count, 2))
    pieces, refs = refs[:places], refs[places:]
    hidden_ref, grad_ref, rows_ref, x_ref, sems, rows_sem = refs
    keep_rows = pltpu.make_async_copy(x_ref, rows_ref, rows_sem)
    step = pl.program_id(0)

    @pl.when(step == 0)
    def _():
        gather_pieces(pieces, x_ref, sems, mine_ref[0], count)
        keep_rows.start()

    hidden = hidden_ref[...]
    for col in range(0, x_ref.shape[1], BLK):
        at = slice(col, col + BLK)
        grad_ref[at, :] = mm(x_ref[:, at], hidden, TN).astype(BF16)

    @pl.when(step == pl.num_programs(0) - 1)
    def _():
        keep_rows.wait()


def down_grad(mine, pieces, hidden, count):
    width = pieces[0].shape[1]
    rows, units = hidden.shape
    return pl.pallas_call(
        functools.partial(down_grad_kernel, count),
        grid=(pl.cdiv(units, BLK),),
        out_shape=(like(width, units), like(rows, width)),
        in_specs=[IN_SMEM]
        + [IN_ANY] * len(pieces)
        + [pl.BlockSpec((rows, BLK), lambda i: (0, i))],
        out_specs=(pl.BlockSpec((width, BLK), lambda i: (0, i)), IN_ANY),
        scratch_shapes=[
            pltpu.VMEM((rows, width), BF16),
            pltpu.SemaphoreType.DMA((len(pieces),)),
            pltpu.SemaphoreType.DMA,
        ],
        compiler_params=PARAMS,
        cost_estimate=cost(2 * rows * width * units, 2 * units * (width + rows)),
        name="down_grad",
    )(mine, *pieces, hidden)


def hidden_grad_kernel(x_ref, w_ref, gate_ref, up_ref, grad_gate_ref, grad_up_ref):
    weights = w_ref[...]
    for row in range(0, x_ref.shape[0], BLK):
        at = slice(row, row + BLK)
        grad = mm(x_ref[at, :], weights)
        grad_gate_ref[at, :] = (grad * gate_ref[at, :].astype(F32)).astype(BF16)
        grad_up_ref[at, :] = (grad * up_ref[at, :].astype(F32)).astype(BF16)


def hidden_grad(cot_rows, full_down, gate_part, up_part):
    rows, width = cot_rows.shape
    units = full_down.shape[1]
    tile = pl.BlockSpec((rows, BLK), lambda i: (0, i))
    return pl.pallas_call(
        hidden_grad_kernel,
        grid=(pl.cdiv(units, BLK),),
        out_shape=(like(rows, units),) * 2,
        in_specs=[
            pl.BlockSpec((rows, width), lambda i: (0, 0)),
            pl.BlockSpec((width, BLK), lambda i: (0, i)),
            tile,
            tile,
        ],
        out_specs=(tile, tile),
        compiler_params=PARAMS,
        cost_estimate=cost(2 * rows * width * units, 2 * units * (width + 4 * rows)),
        name="hidden_grad",
    )(cot_rows, full_down, gate_part, up_part)


def gateup_grad_kernel(x_ref, gate_ref, up_ref, grad_ref):
    owners, _, depth, _ = grad_ref.shape
    for side, part_ref in enumerate((gate_ref, up_ref)):
        part = part_ref[...]
        for col in range(0, x_ref.shape[1], 2 * depth):
            both = mm(x_ref[:, col : col + 2 * depth], part, TN).astype(BF16)
            grad_ref[col // depth, side] = both[:depth]
            grad_ref[col // depth + 1, side] = both[depth:]


def gateup_grad(second_rows, grad_gate, grad_up, owners):
    rows, width = second_rows.shape
    units = grad_gate.shape[1]
    depth = width // owners
    tile = pl.BlockSpec((rows, BLK), lambda i: (0, i))
    return pl.pallas_call(
        gateup_grad_kernel,
        grid=(pl.cdiv(units, BLK),),
        out_shape=like(owners, 2, depth, units),
        in_specs=[pl.BlockSpec((rows, width), lambda i: (0, 0)), tile, tile],
        out_specs=pl.BlockSpec((owners, 2, depth, BLK), lambda i: (0, 0, 0, i)),
        compiler_params=PARAMS,
        cost_estimate=cost(4 * rows * width * units, 4 * units * (width + rows)),
        name="gateup_grad",
    )(second_rows, grad_gate, grad_up)


def attn_grad_kernel(x_ref, mixed_ref, y_ref, out_ref, w_ref, grad_ref, gain_ref):
    qkv_width = mixed_ref.shape[1]
    of_qkv = mm(x_ref[...], mixed_ref[...], TN)
    grad_ref[:, :qkv_width] = of_qkv.astype(BF16)
    grad_ref[:, qkv_width:] = mm(y_ref[...], out_ref[...], TN).astype(BF16)
    high, rest = split_two(of_qkv * w_ref[:, :qkv_width].astype(F32))
    ones = jnp.ones((8, qkv_width), BF16)
    gain_ref[...] = mm(ones, high.astype(BF16), NT) + mm(ones, rest.astype(BF16), NT)


def attn_grad(first_rows, grad_mixed, branch_rows, attended, full_attn):
    rows, width = first_rows.shape
    joined = full_attn.shape[1]
    part = pl.BlockSpec((rows, BLK), lambda i: (0, i))
    whole = lambda values: pl.BlockSpec(values.shape, lambda i: (0, 0))
    return pl.pallas_call(
        attn_grad_kernel,
        grid=(width // BLK,),
        out_shape=(like(width, joined), like(8, width, dtype=F32)),
        in_specs=[
            part,
            whole(grad_mixed),
            part,
            whole(attended),
            pl.BlockSpec((BLK, joined), lambda i: (i, 0)),
        ],
        out_specs=(
            pl.BlockSpec((BLK, joined), lambda i: (i, 0)),
            pl.BlockSpec((8, BLK), lambda i: (0, i)),
        ),
        compiler_params=PARAMS,
        cost_estimate=cost(2 * rows * width * joined, 2 * width * (2 * rows + joined)),
        name="attn_grad",
    )(first_rows, grad_mixed, branch_rows, attended, full_attn)


def tile_halves(groups):
    span = PER + 2
    query = [g * span + j for g in range(groups) for j in range(PER)]
    key = [g * span + PER for g in range(groups)]
    value = [g * span + PER + 1 for g in range(groups)]
    halves = []
    for part in (query, key, value):
        halves += part + [None] * (len(part) % 2)
    return halves


def half_tile(values, idx, side):
    tile = values[:, idx // 2 * LANES : idx // 2 * LANES + LANES]
    if tile.shape[1] < LANES:
        tile = jnp.concatenate([tile, tile], axis=1)
        return tile
    return pltpu.roll(tile, HD, 1) if idx % 2 != side else tile


def reordered(values, halves):
    low = low_lanes(values.shape[0])
    zero = jnp.zeros((values.shape[0], LANES), values.dtype)
    tiles = []
    for first in range(0, len(halves), 2):
        pair = list(halves[first : first + 2])
        parts = [zero if h is None else half_tile(values, h, side) for side, h in enumerate(pair)]
        if len(parts) == 1:
            tiles.append(parts[0][:, :HD])
        else:
            tiles.append(jnp.where(low, parts[0], parts[1]))
    return jnp.concatenate(tiles, axis=1)


def pack_kernel(groups, qkv_ref, out_ref, packed_ref):
    halves = tile_halves(groups)
    qkv_width = len(halves) * HD
    out_width = out_ref.shape[1]
    packed_ref[:, :qkv_width] = reordered(qkv_ref[...], halves).astype(BF16)
    packed_ref[:, qkv_width : qkv_width + out_width] = out_ref[...].astype(BF16)
    tail = packed_ref.shape[1] - qkv_width - out_width
    if tail:
        zeros = jnp.zeros((packed_ref.shape[0], tail), BF16)
        packed_ref[:, qkv_width + out_width :] = zeros


def pack_attn(w_qkv, w_out, groups):
    depth = w_qkv.shape[0]
    q_tiles = (groups * PER + 1) // 2
    width = len(tile_halves(groups)) * HD + q_tiles * LANES
    return pl.pallas_call(
        functools.partial(pack_kernel, groups),
        out_shape=like(depth, width),
        in_specs=[IN_VMEM, IN_VMEM],
        out_specs=IN_VMEM,
        compiler_params=PARAMS,
        name="pack_attn",
    )(w_qkv, w_out)


def attn_step_kernel(groups, grad_ref, *refs):
    halves = tile_halves(groups)
    order = [halves.index(i) for i in range(groups * (PER + 2))]
    qkv_width = len(halves) * HD
    qkv_in, out_in, qkv_out, out_out = refs[:3], refs[3:6], refs[6:9], refs[9:]
    of_qkv = reordered(grad_ref[:, :qkv_width].astype(F32), order)
    of_out = grad_ref[:, qkv_width : qkv_width + out_in[0].shape[1]].astype(F32)
    for grad, old, new in ((of_qkv, qkv_in, qkv_out), (of_out, out_in, out_out)):
        stepped = adamw_step(old[0][...], old[1][...], old[2][...], grad, MATRIX_RATE)
        for ref, values in zip(new, stepped):
            ref[...] = values


def attn_step(grads, qkv, out, groups):
    shapes = [like(*v.shape, dtype=F32) for v in qkv + out]
    return pl.pallas_call(
        functools.partial(attn_step_kernel, groups),
        out_shape=shapes,
        in_specs=[IN_VMEM] * 7,
        out_specs=[IN_VMEM] * 6,
        compiler_params=PARAMS,
        name="attn_step",
    )(grads, *qkv, *out)


def exchange(values, bit, count):
    return lax.ppermute(values, "tensor", [(i, i ^ bit) for i in range(count)])


def near_pieces(own, count):
    return [own] + [exchange(own, j, count) for j in (1, 2) if j < count]


def far_pieces(near, count):
    pieces = list(near)
    bit = len(pieces)
    if count >= 4:
        half = pieces[0].shape[0] // 2
        pieces += [
            exchange(pieces[1][:half], 2, count),
            exchange(pieces[2][half:], 1, count),
        ]
        bit = 4
    while bit < count:
        pieces += [exchange(part, bit, count) for part in pieces]
        bit *= 2
    return pieces


def nothing(sent):
    return sent, ()


def reduce_slots(part_of, count, early=nothing, late=nothing):
    if count < 4:
        total = part_of(0)
        for j in range(1, count):
            total = total + exchange(part_of(j).astype(BF16), j, count).astype(F32)
        return total, early(total)[1], late(total)[1]
    bit = count // 2
    parts = part_of
    while bit >= 4:
        folded = {
            j: exchange(parts(j | bit).astype(BF16), bit, count).astype(F32) + parts(j)
            for j in range(bit)
        }
        parts = folded.__getitem__
        bit //= 2
    far = parts(3).astype(BF16)
    half = far.shape[0] // 2
    far, beside = early(far)
    from_one = exchange(far[:half], 1, count).astype(F32)
    from_two = exchange(far[half:], 2, count).astype(F32)
    second = parts(2)
    first = parts(1)
    second = jnp.concatenate([second[:half] + from_one, second[half:]], axis=0).astype(BF16)
    first = jnp.concatenate([first[:half], first[half:] + from_two], axis=0).astype(BF16)
    first, last = late(first)
    got_two = exchange(second, 2, count)
    got_one = exchange(first, 1, count)
    own = parts(0)
    own, beside, last = tie(own, beside, last)
    return own + got_one.astype(F32) + got_two.astype(F32), beside, last


def tie(*values):
    return lax.optimization_barrier(values)


def body(
    count,
    dp_count,
    tokens,
    cotangent,
    lengths,
    w_qkv,
    m_qkv,
    v_qkv,
    w_out,
    m_out,
    v_out,
    w_gateup,
    m_gateup,
    v_gateup,
    w_down,
    m_down,
    v_down,
    gains,
    m_gains,
    v_gains,
):
    chunk, model_width = tokens.shape
    row_count = chunk * count
    groups = KV // count
    heads = groups * PER
    mine = lax.axis_index("tensor")
    gain_attn = gains[:model_width]
    gain_ffn = gains[model_width : 2 * model_width]
    gain_query = gains[2 * model_width : 2 * model_width + HD]
    gain_key = gains[2 * model_width + HD :]

    def gather_dp(values):
        return lax.all_gather(values, "dp", axis=0, tiled=True)

    def scatter_dp(values):
        return lax.psum_scatter(values, "dp", scatter_dimension=0, tiled=True)

    def slot(values, j):
        return lax.dynamic_slice_in_dim(values, (mine ^ j) * chunk, chunk, 0)

    packed = pack_attn(w_qkv, w_out.T, groups)
    full_attn = gather_dp(packed)
    qkv_width = len(tile_halves(groups)) * HD
    full_qkv = full_attn[:, :qkv_width]
    full_out = full_attn[:, qkv_width:]

    inputs = tokens.astype(F32)
    first_local = norm_rows(inputs, gain_attn).astype(BF16)
    first_local, gateup_local, down_local = tie(first_local, w_gateup, w_down)
    full_gateup = lax.all_gather(gateup_local.astype(BF16), "dp", axis=1, tiled=True)
    full_down = gather_dp(down_local.T.astype(BF16))
    full_gate, full_up = full_gateup[0], full_gateup[1]

    first_pieces = far_pieces(near_pieces(first_local, count), count)
    cotangent, first_pieces = tie(cotangent, first_pieces)
    cot_near = near_pieces(cotangent, count)

    begin_at, positions = layout(lengths[0], row_count)
    cosine, sine_part = angles(positions)
    cos = jnp.concatenate([cosine] * 4, axis=1)
    sin = jnp.concatenate([-sine_part, sine_part] * 2, axis=1)
    own_index = mine[None].astype(jnp.int32)
    scalars = jnp.concatenate([begin_at[::BLK] // BLK, own_index])
    pair_gains = jnp.stack([jnp.tile(gain_query, 2), jnp.tile(gain_key, 2)])
    tables = (cos, sin, pair_gains, begin_at[None, :])

    attended, mixed, first_rows, *saved = attend(
        scalars, first_pieces, full_attn, tables, heads, groups, count
    )
    attended, cot_near = tie(attended, cot_near)

    branch, _, _ = reduce_slots(lambda j: mm(slot(attended, j), full_out, NT), count)
    middle = inputs + branch
    second_local = norm_rows(middle, gain_ffn).astype(BF16)
    second_pieces = far_pieces(near_pieces(second_local, count), count)
    cot_near, second_pieces = tie(cot_near, second_pieces)
    cot_pieces = far_pieces(cot_near, count)

    hidden, gate_part, up_part, second_rows = gateup_forward(
        own_index, second_pieces, full_gateup, count
    )
    grad_down, cot_rows = down_grad(own_index, cot_pieces, hidden, count)
    down_sum = scatter_dp(grad_down)
    grad_gate, grad_up = hidden_grad(cot_rows, full_down, gate_part, up_part)

    def gateup_grads(sent):
        sent, rows = tie(sent, second_rows)
        return sent, gateup_grad(rows, grad_gate, grad_up, dp_count)

    grad_second, _, grad_gateup = reduce_slots(
        lambda j: mm(slot(grad_gate, j), full_gate, NT) + mm(slot(grad_up, j), full_up, NT),
        count,
        late=gateup_grads,
    )
    gateup_sum = scatter_dp(grad_gateup)[0]

    middle_norm, middle_back = jax.vjp(norm_rows, middle, gain_ffn)
    grad_mid_norm, grad_gain_ffn = middle_back(grad_second)
    grad_middle = cotangent.astype(F32) + grad_mid_norm
    grad_branch = grad_middle.astype(BF16)
    branch_near = near_pieces(grad_branch, count)
    branch_near[0], hidden = tie(branch_near[0], hidden)
    shares = [mm(slot(hidden, j), full_down, NT) for j in range(count)]
    branch_pieces = far_pieces(branch_near, count)
    branch_pieces, shares, down_sum = tie(branch_pieces, shares, down_sum)
    shares[1:] = [exchange(v.astype(BF16), j, count) for j, v in enumerate(shares) if j]

    grad_mixed, pair_grads, branch_rows = attend_back(
        scalars, branch_pieces, full_attn, mixed, tables, [attended] + saved, heads, groups, count
    )

    def attn_grads(sent):
        sent, rows = tie(sent, first_rows)
        return sent, attn_grad(rows, grad_mixed, branch_rows, attended, full_attn)

    grad_first, (grad_attn, gain_sums), (gateup_sum, shares) = reduce_slots(
        lambda j: mm(slot(grad_mixed, j), full_qkv, NT),
        count,
        early=attn_grads,
        late=lambda sent: tie(sent, (gateup_sum, shares)),
    )
    output = (middle + sum(v.astype(F32) for v in shares)).astype(BF16)
    attn_sum = scatter_dp(grad_attn)
    pair_sums = pair_grads[:2, :HD] + pair_grads[:2, HD:]
    gain_grads = jnp.concatenate(
        [gain_sums[0] / gain_attn, grad_gain_ffn, pair_sums[0], pair_sums[1]]
    )
    for axis, size in (("tensor", count), ("dp", dp_count)):
        bit = 1
        while bit < size:
            gain_grads = gain_grads + lax.ppermute(
                gain_grads, axis, [(i, i ^ bit) for i in range(size)]
            )
            bit *= 2
    first_norm, first_back = jax.vjp(lambda v: norm_rows(v, gain_attn), inputs)
    grad_tokens = grad_middle + first_back(grad_first)[0]

    turned = lambda values: [v.T for v in values]
    stepped = attn_step(
        attn_sum, [w_qkv, m_qkv, v_qkv], turned([w_out, m_out, v_out]), groups
    )
    gateup_new = adamw_step(w_gateup, m_gateup, v_gateup, gateup_sum.astype(F32), MATRIX_RATE)
    down_new = adamw_step(w_down.T, m_down.T, v_down.T, down_sum.astype(F32), MATRIX_RATE)
    gains_new = adamw_step(gains, m_gains, v_gains, gain_grads, GAIN_RATE)
    return (
        (output, grad_tokens)
        + tuple(stepped[:3])
        + tuple(turned(stepped[3:]))
        + gateup_new
        + tuple(turned(down_new))
        + gains_new
    )


def solution(mesh):
    rows = P(("dp", "tensor"), None)
    qkv = P("dp", "tensor")
    turned = P("tensor", "dp")
    gateup = P(None, "dp", "tensor")
    weights = (qkv,) * 3 + (turned,) * 3 + (gateup,) * 3 + (turned,) * 3 + (P(),) * 3
    return jax.shard_map(
        functools.partial(body, mesh.shape["tensor"], mesh.shape["dp"]),
        mesh=mesh,
        in_specs=(rows, rows, P("dp", None)) + weights,
        out_specs=(rows, rows) + weights,
        check_vma=False,
    )
```

```python
import functools
import math

import jax
import jax.numpy as jnp
from jax import lax
from jax.experimental import pallas as pl
from jax.experimental.pallas import tpu as pltpu
from jax.sharding import PartitionSpec as P

HEADS = 24
KV = 8
HD = 64
STEP = 10
PER = HEADS // KV

NORM_EPS = 1e-05
ROPE_BASE = 1000000.0
BETA_ONE = 0.9
BETA_TWO = 0.95
ADAM_EPS = 1e-08
WEIGHT_DECAY = 0.1
MATRIX_RATE = 0.05
GAIN_RATE = 0.5

LANES = 128
BLK = 256
LOG2E = math.log2(math.e)
BF16 = jnp.bfloat16
F32 = jnp.float32
NN = (((1,), (0,)), ((), ()))
NT = (((1,), (1,)), ((), ()))
TN = (((0,), (0,)), ((), ()))


def mm(left, right, dims=NN):
    return lax.dot_general(left, right, dims, preferred_element_type=F32)


def norm_rows(values, gain):
    return values * lax.rsqrt(jnp.mean(values * values, axis=-1, keepdims=True) + NORM_EPS) * gain


def layout(counts, row_count):
    ends_at = jnp.cumsum(counts)
    starts = ends_at - counts
    place_idx = jnp.arange(row_count, dtype=jnp.int32)
    owners = jnp.sum((place_idx[:, None] >= ends_at[None, :]).astype(jnp.int32), axis=1)
    slots = jnp.arange(counts.shape[0], dtype=jnp.int32)
    return jnp.sum(jnp.where(owners[:, None] == slots[None, :], starts[None, :], 0), axis=1)


def tables_kernel(counts_ref, turn_ref, sign_ref, cos_ref, sin_ref):
    def step(blk, _):
        at = pl.ds(pl.multiple_of(blk * BLK, BLK), BLK)
        places = blk * BLK + lax.broadcasted_iota(jnp.int32, (BLK, LANES), 0)
        positions = places
        end = 0
        for idx in range(counts_ref.shape[1]):
            count = counts_ref[0, idx]
            end = end + count
            positions = positions - jnp.where(places >= end, count, 0)
        turn = positions.astype(F32) * turn_ref[...]
        cos_ref[at, :] = jnp.cos(turn)
        sin_ref[at, :] = jnp.sin(turn) * sign_ref[...]
        return 0

    lax.fori_loop(0, cos_ref.shape[0] // BLK, step, 0)


def make_tables(counts, rows):
    lane = jnp.arange(LANES) % HD
    half_width = HD // 2
    turn = ROPE_BASE ** (-((lane % half_width).astype(F32) * 2.0 / HD))
    sign = jnp.where(lane < half_width, -1.0, 1.0).astype(F32)
    return pl.pallas_call(
        tables_kernel,
        out_shape=(like(rows, LANES, dtype=F32),) * 2,
        in_specs=[IN_SMEM, IN_VMEM, IN_VMEM],
        out_specs=(IN_VMEM, IN_VMEM),
        cost_estimate=BESIDE,
        name="tables",
    )(counts, turn[None, :], sign[None, :])


def adamw_step(weight, first_old, second_old, gradient, step_rate):
    first_new = BETA_ONE * first_old + (1.0 - BETA_ONE) * gradient
    second_new = BETA_TWO * second_old + (1.0 - BETA_TWO) * gradient * gradient
    first_fixed = first_new / (1.0 - BETA_ONE**STEP)
    second_fixed = second_new / (1.0 - BETA_TWO**STEP)
    weight_new = weight - step_rate * (
        first_fixed / (jnp.sqrt(second_fixed) + ADAM_EPS) + WEIGHT_DECAY * weight
    )
    return (weight_new, first_new, second_new)


def piece_rows(pieces, chunk, mine=None):
    rows = []
    at = 0
    for piece in pieces:
        slot, off = divmod(at, chunk)
        if mine is None:
            rows.append(at)
        else:
            rows.append(pl.multiple_of(jnp.bitwise_xor(mine, slot) * chunk + off, chunk // 2))
        at += piece.shape[0]
    return rows


def half_sums(values):
    row = lax.broadcasted_iota(jnp.int32, (LANES, LANES), 0) // HD
    col = lax.broadcasted_iota(jnp.int32, (LANES, LANES), 1) // HD
    return mm(values.astype(BF16), jnp.where(row == col, 1.0, 0.0).astype(BF16))


def swap_halves(values):
    lane = lax.broadcasted_iota(jnp.int32, values.shape, 1)
    half = HD // 2
    return jnp.where(
        (lane % HD) < half, pltpu.roll(values, LANES - half, 1), pltpu.roll(values, half, 1)
    )


def split_two(values):
    high = values.astype(BF16).astype(F32)
    return high, values - high


def low_lanes(rows):
    return lax.broadcasted_iota(jnp.int32, (rows, LANES), 1) < HD


def turn_blocks(src_ref, dst_ref):
    def step(blk, _):
        at = pl.ds(pl.multiple_of(blk * BLK, BLK), BLK)
        for group in range(src_ref.shape[0]):
            turned = jnp.transpose(src_ref[group, at, :].astype(F32))
            dst_ref[group, :, at] = turned.astype(BF16)
        return 0

    lax.fori_loop(0, src_ref.shape[1] // BLK, step, 0)


class Copies:
    def __init__(self, sems):
        self.sems = sems
        self.used = 0
        self.open = []

    def start(self, src, dst):
        copy = pltpu.make_async_copy(src, dst, self.sems.at[self.used])
        self.used += 1
        copy.start()
        self.open.append(copy)
        return copy

    def wait(self, *copies):
        copies = copies or tuple(self.open)
        for copy in copies:
            copy.wait()
        self.open = [own for own in self.open if all(own is not copy for copy in copies)]


def store_shares(copies, share_refs, own_buf, part_buf, count, mine, share_of):
    half = part_buf.shape[1]
    for slot in reversed(range(count)):
        row = pl.multiple_of(jnp.bitwise_xor(mine, slot) * (2 * half), 2 * half)
        for side in range(2):
            share = share_of(pl.multiple_of(row + side * half, half), half)
            if slot == 0:
                own = slice(side * half, (side + 1) * half)
                own_buf[own, :] = share
                copies.start(own_buf.at[own, :], share_refs[0].at[own, :])
            else:
                idx = 2 * slot - 2 + side
                part_buf[idx] = share.astype(BF16)
                copies.start(part_buf.at[idx], share_refs[idx + 1])


def fwd_kernel(heads, groups, count, scalars, *refs):
    pieces, refs = refs[: 2 * count], refs[2 * count :]
    w_ref, cos_ref, sin_ref, gains_ref, start_ref = refs[:5]
    shares, refs = refs[5 : 4 + 2 * count], refs[4 + 2 * count :]
    kept_refs, rows_ref, refs = refs[:5], refs[5], refs[6:]
    out_ref, mixed_ref, qaug_ref, kaug_ref, vaug_ref = refs[:5]
    own_buf, part_buf, vt_ref, acc_ref, sems = refs[5:]
    copies = Copies(sems)
    rows = mixed_ref.shape[0]
    q_tiles = (heads + 1) // 2
    k_tiles = (groups + 1) // 2
    qkv_width = mixed_ref.shape[1]
    mine = scalars[rows // BLK]

    def prep(x_ref, row):
        size = x_ref.shape[0]
        at = pl.ds(row, size)
        cos = cos_ref[at, :]
        sin = sin_ref[at, :]
        lane = lax.broadcasted_iota(jnp.int32, (size, LANES), 1)
        low = lane < HD
        mixed = mm(x_ref[...], w_ref[:, :qkv_width])
        mixed_ref[at, :] = mixed

        def turned(tile, which):
            raw = mixed[:, tile * LANES : (tile + 1) * LANES]
            scaled = raw * lax.rsqrt(half_sums(raw * raw) * (1.0 / HD) + NORM_EPS)
            scaled = scaled * gains_ref[which : which + 1, :]
            return scaled * cos + swap_halves(scaled) * sin

        for tile in range(q_tiles):
            query = turned(tile, 0) * (LOG2E * HD**-0.5)
            qaug_ref[2 * tile, at, :] = jnp.where(low, query, 0.0).astype(BF16)
            if 2 * tile + 1 < heads:
                other = jnp.where(low, pltpu.roll(query, HD, 1), 0.0)
                qaug_ref[2 * tile + 1, at, :] = other.astype(BF16)
        ones = jnp.where((lane == HD) | (lane == HD + 1), 1.0, 0.0)
        for tile in range(k_tiles):
            key = turned(q_tiles + tile, 1)
            v_at = (q_tiles + k_tiles + tile) * LANES
            value = mixed[:, v_at : v_at + LANES]
            for side in range(min(2, groups - 2 * tile)):
                if side:
                    key = pltpu.roll(key, HD, 1)
                    value = pltpu.roll(value, HD, 1)
                own_value = jnp.where(low, value, ones)
                kaug_ref[2 * tile + side, at, :] = jnp.where(low, key, ones).astype(BF16)
                vaug_ref[2 * tile + side, at, :] = own_value.astype(BF16)

    for idx, row in enumerate(piece_rows(pieces, rows // count, mine)):
        copies.start(pieces[idx], rows_ref.at[pl.ds(row, pieces[idx].shape[0]), :])
        prep(pieces[idx], row)
    for idx, ref in enumerate((mixed_ref, kaug_ref, vaug_ref)):
        copies.start(ref, kept_refs[(1, 3, 4)[idx]])
    turn_blocks(vaug_ref, vt_ref)
    key_idx = lax.broadcasted_iota(jnp.int32, (BLK, BLK), 0)
    ahead = key_idx - lax.broadcasted_iota(jnp.int32, (BLK, BLK), 1)

    def per_query(q_blk, _):
        q_at = pl.ds(pl.multiple_of(q_blk * BLK, BLK), BLK)
        acc_ref[...] = jnp.zeros_like(acc_ref)
        start = start_ref[0:1, q_at]

        def per_key(k_blk, _):
            k_at = pl.ds(pl.multiple_of(k_blk * BLK, BLK), BLK)
            admitted = (key_idx >= start - k_blk * BLK) & (ahead <= (q_blk - k_blk) * BLK)
            for group in range(groups):
                query = qaug_ref[group * PER : (group + 1) * PER, q_at, :]
                scores = mm(kaug_ref[group, k_at, :], query.reshape(PER * BLK, LANES), NT)
                probs = [
                    jnp.where(admitted, jnp.exp2(scores[:, j * BLK : (j + 1) * BLK]), 0.0)
                    for j in range(PER)
                ]
                probs = jnp.concatenate([p.astype(BF16) for p in probs], axis=1)
                acc_ref[group] += mm(vt_ref[group, :, k_at], probs)
            return 0

        lax.fori_loop(scalars[q_blk], q_blk + 1, per_key, 0)
        low = low_lanes(BLK)
        kept = None
        for head in range(heads):
            raw = acc_ref[head // PER, :, (head % PER) * BLK : (head % PER + 1) * BLK]
            total = raw[HD : HD + 1, :]
            high, rest = split_two(jnp.log2(total))
            sub = lax.broadcasted_iota(jnp.int32, raw.shape, 0)
            tail = jnp.where(sub == HD, -high, jnp.where(sub == HD + 1, -rest, 0.0))
            whole = jnp.transpose(jnp.where(sub < HD, raw * (1.0 / total), tail))
            query = qaug_ref[head, q_at, :].astype(F32)
            qaug_ref[head, q_at, :] = jnp.where(low, query, whole).astype(BF16)
            if head % 2 == 0:
                kept = whole
            if head % 2 == 1 or head == heads - 1:
                second = pltpu.roll(whole, HD, 1) if head % 2 == 1 else jnp.zeros_like(whole)
                cols = slice(head // 2 * LANES, (head // 2 + 1) * LANES)
                out_ref[q_at, cols] = jnp.where(low, kept, second).astype(BF16)
        return 0

    lax.fori_loop(0, rows // BLK, per_query, 0)

    copies.start(out_ref, kept_refs[0])
    copies.start(qaug_ref, kept_refs[2])

    def share(row, size):
        return mm(out_ref[pl.ds(row, size), :], w_ref[:, qkv_width:], NT)

    store_shares(copies, shares, own_buf, part_buf, count, mine, share)
    copies.wait()


def bwd_kernel(heads, groups, count, scalars, *refs):
    pieces, refs = refs[: 2 * count], refs[2 * count :]
    gains_ref, start_ref = refs[:2]
    given, refs = refs[2:10], refs[10:]
    shares, refs = refs[: 2 * count - 1], refs[2 * count - 1 :]
    gm_out, gg_ref, rows_ref = refs[:3]
    w_ref, out_ref, kaug_ref, vaug_ref, qaug_ref, mixed_ref, cos_ref, sin_ref = refs[3:11]
    gm_ref, own_buf, part_buf, daug_ref, kt_ref, dq_ref, dk_ref, dv_ref, sems = refs[11:]
    copies = Copies(sems)
    loads = [copies.start(src, dst) for src, dst in zip(given, refs[3:11])]
    rows = mixed_ref.shape[0]
    q_tiles = (heads + 1) // 2
    k_tiles = (groups + 1) // 2
    qkv_width = mixed_ref.shape[1]
    mine = scalars[rows // BLK]

    def prep(x_ref, row):
        size = x_ref.shape[0]
        at = pl.ds(row, size)
        lane = lax.broadcasted_iota(jnp.int32, (size, LANES), 1)
        low = lane < HD
        grads = mm(x_ref[...], w_ref[:, qkv_width:]).astype(BF16).astype(F32)
        for tile in range(q_tiles):
            grad = grads[:, tile * LANES : (tile + 1) * LANES]
            out = out_ref[at, tile * LANES : (tile + 1) * LANES].astype(F32)
            high, rest = split_two(-half_sums(grad * out))
            tail = jnp.where(lane % HD == 0, high, jnp.where(lane % HD == 1, rest, 0.0))
            daug_ref[2 * tile, at, :] = jnp.where(low, grad, pltpu.roll(tail, HD, 1)).astype(BF16)
            if 2 * tile + 1 < heads:
                other = jnp.where(low, pltpu.roll(grad, HD, 1), tail)
                daug_ref[2 * tile + 1, at, :] = other.astype(BF16)

    for idx, row in enumerate(piece_rows(pieces, rows // count, mine)):
        copies.start(pieces[idx], rows_ref.at[pl.ds(row, pieces[idx].shape[0]), :])
        if idx == 0:
            copies.wait(*loads[:2])
        prep(pieces[idx], row)
    copies.wait(*loads[2:])
    turn_blocks(kaug_ref, kt_ref)
    dk_ref[...] = jnp.zeros_like(dk_ref)
    dv_ref[...] = jnp.zeros_like(dv_ref)
    gg_ref[...] = jnp.zeros_like(gg_ref)
    key_idx = lax.broadcasted_iota(jnp.int32, (BLK, BLK), 0)
    ahead = key_idx - lax.broadcasted_iota(jnp.int32, (BLK, BLK), 1)

    def finish(at, tile, which, grad):
        cols = slice(tile * LANES, (tile + 1) * LANES)
        raw = mixed_ref[at, cols]
        back = grad * cos_ref[at, :] - swap_halves(grad) * sin_ref[at, :]
        scale = lax.rsqrt(half_sums(raw * raw) * (1.0 / HD) + NORM_EPS)
        unscaled = raw * scale
        gg_ref[which : which + 1, :] += jnp.sum(back * unscaled, axis=0, keepdims=True)
        back = back * gains_ref[which : which + 1, :]
        mean = half_sums(unscaled * back) * (1.0 / HD)
        gm_ref[at, cols] = (scale * (back - unscaled * mean)).astype(BF16)

    def per_query(q_blk, _):
        q_at = pl.ds(pl.multiple_of(q_blk * BLK, BLK), BLK)
        start = start_ref[0:1, q_at]
        dq_ref[...] = jnp.zeros_like(dq_ref)

        def per_key(k_blk, _):
            k_at = pl.ds(pl.multiple_of(k_blk * BLK, BLK), BLK)
            admitted = (key_idx >= start - k_blk * BLK) & (ahead <= (q_blk - k_blk) * BLK)
            for group in range(groups):
                own = slice(group * PER, (group + 1) * PER)
                query = qaug_ref[own, q_at, :].reshape(PER * BLK, LANES)
                grad = daug_ref[own, q_at, :].reshape(PER * BLK, LANES)
                scores = mm(kaug_ref[group, k_at, :], query, NT)
                grad_probs = mm(vaug_ref[group, k_at, :], grad, NT)
                probs, grad_scores = [], []
                for j in range(PER):
                    cols = slice(j * BLK, (j + 1) * BLK)
                    prob = jnp.where(admitted, jnp.exp2(scores[:, cols]), 0.0)
                    probs.append(prob.astype(BF16))
                    grad_scores.append((prob * grad_probs[:, cols]).astype(BF16))
                probs = jnp.concatenate(probs, axis=1)
                grad_scores = jnp.concatenate(grad_scores, axis=1)
                dv_ref[group, k_at, :] += mm(probs, grad)
                dk_ref[group, k_at, :] += mm(grad_scores, query)
                dq_ref[group] += mm(kt_ref[group, :, k_at], grad_scores)
            return 0

        lax.fori_loop(scalars[q_blk], q_blk + 1, per_key, 0)
        low = low_lanes(BLK)
        for tile in range(q_tiles):
            pair = []
            for head in range(2 * tile, 2 * tile + 2):
                if head < heads:
                    cols = slice((head % PER) * BLK, (head % PER + 1) * BLK)
                    own = jnp.transpose(dq_ref[head // PER, :, cols])
                    pair.append(pltpu.roll(own, HD, 1) if head % 2 else own)
                else:
                    pair.append(jnp.zeros((BLK, LANES), F32))
            finish(q_at, tile, 0, jnp.where(low, pair[0], pair[1]) * HD**-0.5)
        return 0

    lax.fori_loop(0, rows // BLK, per_query, 0)

    def per_key_block(blk, _):
        at = pl.ds(pl.multiple_of(blk * BLK, BLK), BLK)
        low = low_lanes(BLK)

        def joined(ref, tile):
            first = ref[2 * tile, at, :]
            if 2 * tile + 1 < groups:
                return jnp.where(low, first, pltpu.roll(ref[2 * tile + 1, at, :], HD, 1))
            return jnp.where(low, first, 0.0)

        for tile in range(k_tiles):
            finish(at, q_tiles + tile, 1, joined(dk_ref, tile) * (1.0 / LOG2E))
            v_at = (q_tiles + k_tiles + tile) * LANES
            gm_ref[at, v_at : v_at + LANES] = joined(dv_ref, tile).astype(BF16)
        return 0

    lax.fori_loop(0, rows // BLK, per_key_block, 0)

    copies.start(gm_ref, gm_out)

    def share(row, size):
        return mm(gm_ref[pl.ds(row, size), :], w_ref[:, :qkv_width], NT)

    store_shares(copies, shares, own_buf, part_buf, count, mine, share)
    copies.wait()


IN_VMEM = pl.BlockSpec(memory_space=pltpu.VMEM)
IN_SMEM = pl.BlockSpec(memory_space=pltpu.SMEM)
IN_ANY = pl.BlockSpec(memory_space=pl.ANY)


def vmem(mib):
    return pltpu.CompilerParams(vmem_limit_bytes=mib * 1024 * 1024)


def like(*shape, dtype=BF16):
    return jax.ShapeDtypeStruct(shape, dtype)


def cost(flops, moved, special=0):
    return pl.CostEstimate(flops=flops, bytes_accessed=moved, transcendentals=special)


def share_shapes(chunk, width, count):
    return [like(chunk, width, dtype=F32)] + [like(chunk // 2, width)] * (2 * count - 2)


BESIDE = cost(10**6, 10**6)


def attend(scalars, pieces, full_attn, tables, heads, groups, count):
    half, width = pieces[0].shape
    rows = 2 * half * count
    q_tiles, k_tiles = (heads + 1) // 2, (groups + 1) // 2
    qkv_width = (q_tiles + 2 * k_tiles) * LANES
    pairs = heads * rows * rows
    shares = share_shapes(2 * half, width, count)
    kept = [
        like(rows, q_tiles * LANES),
        like(rows, qkv_width, dtype=F32),
        like(heads, rows, LANES),
        like(groups, rows, LANES),
        like(groups, rows, LANES),
    ]
    results = pl.pallas_call(
        functools.partial(fwd_kernel, heads, groups, count),
        out_shape=shares + kept + [like(rows, width)],
        in_specs=[IN_SMEM] + [IN_VMEM] * (len(pieces) + 5),
        out_specs=[IN_ANY] * (len(shares) + len(kept) + 1),
        scratch_shapes=[pltpu.VMEM(v.shape, v.dtype) for v in kept]
        + [
            pltpu.VMEM((2 * half, width), F32),
            pltpu.VMEM((2 * count - 2, half, width), BF16),
            pltpu.VMEM((groups, LANES, rows), BF16),
            pltpu.VMEM((groups, LANES, PER * BLK), F32),
            pltpu.SemaphoreType.DMA((4 * count + 5,)),
        ],
        compiler_params=vmem(48),
        cost_estimate=cost(8 * pairs * LANES, 8 * rows * width, pairs),
        name="attend",
    )(scalars, *pieces, full_attn, *tables)
    return results[: len(shares)], results[len(shares) :]


def attend_back(scalars, pieces, full_attn, mixed, tables, saved, heads, groups, count):
    half, width = pieces[0].shape
    rows = 2 * half * count
    pairs = heads * rows * rows
    shares = share_shapes(2 * half, width, count)
    cos, sin, pair_gains, start = tables
    attended, qaug, kaug, vaug = saved
    given = [full_attn, attended, kaug, vaug, qaug, mixed, cos, sin]
    results = pl.pallas_call(
        functools.partial(bwd_kernel, heads, groups, count),
        out_shape=shares
        + [like(*mixed.shape), like(8, LANES, dtype=F32), like(rows, width)],
        in_specs=[IN_SMEM] + [IN_VMEM] * (len(pieces) + 2) + [IN_ANY] * len(given),
        out_specs=[IN_ANY] * len(shares) + [IN_ANY, IN_VMEM, IN_ANY],
        scratch_shapes=[pltpu.VMEM(v.shape, v.dtype) for v in given]
        + [
            pltpu.VMEM(mixed.shape, BF16),
            pltpu.VMEM((2 * half, width), F32),
            pltpu.VMEM((2 * count - 2, half, width), BF16),
            pltpu.VMEM((heads, rows, LANES), BF16),
            pltpu.VMEM((groups, LANES, rows), BF16),
            pltpu.VMEM((groups, LANES, PER * BLK), F32),
            pltpu.VMEM((groups, rows, LANES), F32),
            pltpu.VMEM((groups, rows, LANES), F32),
            pltpu.SemaphoreType.DMA((4 * count + len(given) + 1,)),
        ],
        compiler_params=vmem(48),
        cost_estimate=cost(12 * pairs * LANES, 8 * rows * width, pairs),
        name="attend_back",
    )(scalars, *pieces, pair_gains, start, *given)
    return results[: len(shares)], results[len(shares) :]


def gateup_kernel(count, *refs):
    pieces, refs = refs[: 2 * count], refs[2 * count :]
    w_ref, hidden_ref, gate_ref, up_ref, rows_ref, sems = refs
    step = pl.program_id(0)
    rows = piece_rows(pieces, 2 * pieces[0].shape[0])
    copies = [
        pltpu.make_async_copy(piece, rows_ref.at[pl.ds(row, piece.shape[0]), :], sems.at[idx])
        for idx, (piece, row) in enumerate(zip(pieces, rows))
    ]

    @pl.when(step == 0)
    def _():
        for keep in copies:
            keep.start()

    w_gate = w_ref[0]
    w_up = w_ref[1]
    for piece, row in zip(pieces, rows):
        at = slice(row, row + piece.shape[0])
        gate = mm(piece[...], w_gate)
        up = mm(piece[...], w_up)
        sigmoid = jax.nn.sigmoid(gate)
        silu = gate * sigmoid
        hidden_ref[at, :] = (silu * up).astype(BF16)
        gate_ref[at, :] = (up * sigmoid * (1.0 + (gate - silu))).astype(BF16)
        up_ref[at, :] = silu.astype(BF16)

    @pl.when(step == pl.num_programs(0) - 1)
    def _():
        for keep in copies:
            keep.wait()


def gateup_forward(pieces, full_gateup, count):
    half, width = pieces[0].shape
    rows = 2 * half * count
    units = full_gateup.shape[2]
    tile = pl.BlockSpec((rows, BLK), lambda i: (0, i))
    return pl.pallas_call(
        functools.partial(gateup_kernel, count),
        grid=(pl.cdiv(units, BLK),),
        out_shape=(like(rows, units),) * 3 + (like(rows, width),),
        in_specs=[IN_VMEM] * len(pieces) + [pl.BlockSpec((2, width, BLK), lambda i: (0, 0, i))],
        out_specs=(tile, tile, tile, IN_ANY),
        scratch_shapes=[pltpu.SemaphoreType.DMA((len(pieces),))],
        compiler_params=vmem(48),
        cost_estimate=cost(4 * rows * width * units, 2 * units * (2 * width + 3 * rows)),
        name="gateup",
    )(*pieces, full_gateup)


def down_grad_kernel(count, *refs):
    pieces, (hidden_ref, grad_ref) = refs[:count], refs[count:]
    chunk = pieces[0].shape[0]
    for col in range(0, grad_ref.shape[0], BLK):
        at = slice(col, col + BLK)
        total = 0.0
        for slot, piece in enumerate(pieces):
            total += mm(piece[:, at], hidden_ref[slot * chunk : (slot + 1) * chunk, :], TN)
        grad_ref[at, :] = total.astype(BF16)


def down_grad(pieces, hidden, count):
    width = pieces[0].shape[1]
    rows, units = hidden.shape
    return pl.pallas_call(
        functools.partial(down_grad_kernel, count),
        grid=(pl.cdiv(units, BLK),),
        out_shape=like(width, units),
        in_specs=[IN_VMEM] * len(pieces) + [pl.BlockSpec((rows, BLK), lambda i: (0, i))],
        out_specs=pl.BlockSpec((width, BLK), lambda i: (0, i)),
        compiler_params=vmem(48),
        cost_estimate=cost(2 * rows * width * units, 2 * units * (width + rows)),
        name="down_grad",
    )(*pieces, hidden)


def hidden_grad_kernel(count, *refs):
    pieces, refs = refs[:count], refs[count:]
    w_ref, gate_ref, up_ref, grad_gate_ref, grad_up_ref = refs
    weights = w_ref[...]
    chunk = pieces[0].shape[0]
    for slot, piece in enumerate(pieces):
        at = slice(slot * chunk, (slot + 1) * chunk)
        grad = mm(piece[...], weights)
        grad_gate_ref[at, :] = (grad * gate_ref[at, :].astype(F32)).astype(BF16)
        grad_up_ref[at, :] = (grad * up_ref[at, :].astype(F32)).astype(BF16)


def hidden_grad(pieces, full_down, gate_part, up_part, count):
    width = pieces[0].shape[1]
    rows, units = gate_part.shape
    tile = pl.BlockSpec((rows, BLK), lambda i: (0, i))
    return pl.pallas_call(
        functools.partial(hidden_grad_kernel, count),
        grid=(pl.cdiv(units, BLK),),
        out_shape=(like(rows, units),) * 2,
        in_specs=[IN_VMEM] * len(pieces)
        + [pl.BlockSpec((width, BLK), lambda i: (0, i)), tile, tile],
        out_specs=(tile, tile),
        compiler_params=vmem(48),
        cost_estimate=cost(2 * rows * width * units, 2 * units * (width + 4 * rows)),
        name="hidden_grad",
    )(*pieces, full_down, gate_part, up_part)


def second_kernel(slots, *refs):
    grads, (w_ref,), outs = refs[: 2 * slots], refs[2 * slots : 2 * slots + 1], refs[2 * slots + 1 :]
    for idx in range(slots):
        total = mm(grads[2 * idx][...], w_ref[0], NT) + mm(grads[2 * idx + 1][...], w_ref[1], NT)
        if len(outs) == slots:
            outs[idx][...] = total
        else:
            half = total.shape[0] // 2
            outs[2 * idx][...] = total[:half].astype(BF16)
            outs[2 * idx + 1][...] = total[half:].astype(BF16)


def second_shares(slots, grad_gate, grad_up, full_gateup, chunk):
    _, width, units = full_gateup.shape
    cols = 2 * BLK
    own = list(slots) == [0]
    rows_of = [pl.BlockSpec((chunk, units), lambda i, j=j: (j, 0)) for j in slots for _ in (0, 1)]
    height = chunk if own else chunk // 2
    outs = len(slots) * (1 if own else 2)
    return pl.pallas_call(
        functools.partial(second_kernel, len(slots)),
        grid=(width // cols,),
        out_shape=[like(height, width, dtype=F32 if own else BF16)] * outs,
        in_specs=rows_of + [pl.BlockSpec((2, cols, units), lambda i: (0, i, 0))],
        out_specs=[pl.BlockSpec((height, cols), lambda i: (0, i))] * outs,
        compiler_params=vmem(48),
        cost_estimate=BESIDE,
        name="second_share",
    )(*([grad_gate, grad_up] * len(slots)), full_gateup)


def down_share_kernel(hidden_ref, w_ref, *outs):
    chunk = outs[0].shape[0]
    for slot, out in enumerate(outs):
        rows = slice(slot * chunk, (slot + 1) * chunk)
        out[...] = mm(hidden_ref[rows, :], w_ref[...], NT).astype(out.dtype)


def down_shares(hidden, full_down, count):
    rows, units = hidden.shape
    width = full_down.shape[0]
    chunk, cols = rows // count, 2 * BLK
    return pl.pallas_call(
        down_share_kernel,
        grid=(width // cols,),
        out_shape=[like(chunk, width, dtype=F32)] + [like(chunk, width)] * (count - 1),
        in_specs=[
            pl.BlockSpec((rows, units), lambda i: (0, 0)),
            pl.BlockSpec((cols, units), lambda i: (i, 0)),
        ],
        out_specs=[pl.BlockSpec((chunk, cols), lambda i: (0, i))] * count,
        compiler_params=vmem(48),
        cost_estimate=BESIDE,
        name="down_share",
    )(hidden, full_down)


def gateup_grad_kernel(x_ref, gate_ref, up_ref, grad_ref):
    _, _, depth, _ = grad_ref.shape
    for side, part_ref in enumerate((gate_ref, up_ref)):
        part = part_ref[...]
        for col in range(0, x_ref.shape[1], 2 * depth):
            both = mm(x_ref[:, col : col + 2 * depth], part, TN).astype(BF16)
            grad_ref[col // depth, side] = both[:depth]
            grad_ref[col // depth + 1, side] = both[depth:]


def gateup_grad(second_rows, grad_gate, grad_up, owners):
    rows, width = second_rows.shape
    units = grad_gate.shape[1]
    depth = width // owners
    tile = pl.BlockSpec((rows, BLK), lambda i: (0, i))
    return pl.pallas_call(
        gateup_grad_kernel,
        grid=(pl.cdiv(units, BLK),),
        out_shape=like(owners, 2, depth, units),
        in_specs=[pl.BlockSpec((rows, width), lambda i: (0, 0)), tile, tile],
        out_specs=pl.BlockSpec((owners, 2, depth, BLK), lambda i: (0, 0, 0, i)),
        compiler_params=vmem(48),
        cost_estimate=BESIDE,
        name="gateup_grad",
    )(second_rows, grad_gate, grad_up)


def attn_grad_kernel(x_ref, mixed_ref, y_ref, out_ref, w_ref, grad_ref, gain_ref):
    qkv_width = mixed_ref.shape[1]
    of_qkv = mm(x_ref[...], mixed_ref[...], TN)
    grad_ref[:, :qkv_width] = of_qkv.astype(BF16)
    grad_ref[:, qkv_width:] = mm(y_ref[...], out_ref[...], TN).astype(BF16)
    high, rest = split_two(of_qkv * w_ref[:, :qkv_width].astype(F32))
    ones = jnp.ones((8, qkv_width), BF16)
    gain_ref[...] = mm(ones, high.astype(BF16), NT) + mm(ones, rest.astype(BF16), NT)


def attn_grad(first_rows, grad_mixed, branch_rows, attended, full_attn):
    rows, width = first_rows.shape
    joined = full_attn.shape[1]
    part = pl.BlockSpec((rows, BLK), lambda i: (0, i))
    whole = lambda values: pl.BlockSpec(values.shape, lambda i: (0, 0))
    return pl.pallas_call(
        attn_grad_kernel,
        grid=(width // BLK,),
        out_shape=(like(width, joined), like(8, width, dtype=F32)),
        in_specs=[
            part,
            whole(grad_mixed),
            part,
            whole(attended),
            pl.BlockSpec((BLK, joined), lambda i: (i, 0)),
        ],
        out_specs=(
            pl.BlockSpec((BLK, joined), lambda i: (i, 0)),
            pl.BlockSpec((8, BLK), lambda i: (0, i)),
        ),
        compiler_params=vmem(48),
        cost_estimate=BESIDE,
        name="attn_grad",
    )(first_rows, grad_mixed, branch_rows, attended, full_attn)


def pack_gains_kernel(attn_ref, gains_ref, ffn_ref, pair_ref, out_ref):
    width = ffn_ref.shape[1]
    out_ref[:, :width] = attn_ref[0:1, :] / gains_ref[:, :width]
    out_ref[:, width : 2 * width] = ffn_ref[...]
    pair = pair_ref[0:2, :]
    pair = pair + pltpu.roll(pair, HD, 1)
    out_ref[:, 2 * width :] = jnp.where(low_lanes(1), pair[0:1], pair[1:2])


def pack_gains(attn_sums, gains, grad_ffn, pair_grads):
    return pl.pallas_call(
        pack_gains_kernel,
        out_shape=like(1, gains.shape[0], dtype=F32),
        in_specs=[IN_VMEM] * 4,
        out_specs=IN_VMEM,
        name="pack_gains",
    )(attn_sums, gains[None, :], grad_ffn, pair_grads)


def tile_halves(groups):
    span = PER + 2
    query = [g * span + j for g in range(groups) for j in range(PER)]
    key = [g * span + PER for g in range(groups)]
    value = [g * span + PER + 1 for g in range(groups)]
    halves = []
    for part in (query, key, value):
        halves += part + [None] * (len(part) % 2)
    return halves


def half_tile(values, idx, side):
    tile = values[:, idx // 2 * LANES : idx // 2 * LANES + LANES]
    if tile.shape[1] < LANES:
        tile = jnp.concatenate([tile, tile], axis=1)
        return tile
    return pltpu.roll(tile, HD, 1) if idx % 2 != side else tile


def reordered(values, halves):
    low = low_lanes(values.shape[0])
    zero = jnp.zeros((values.shape[0], LANES), values.dtype)
    tiles = []
    for first in range(0, len(halves), 2):
        pair = list(halves[first : first + 2])
        parts = [zero if h is None else half_tile(values, h, side) for side, h in enumerate(pair)]
        if len(parts) == 1:
            tiles.append(parts[0][:, :HD])
        else:
            tiles.append(jnp.where(low, parts[0], parts[1]))
    return jnp.concatenate(tiles, axis=1)


def pack_kernel(groups, qkv_ref, out_ref, packed_ref):
    halves = tile_halves(groups)
    qkv_width = len(halves) * HD
    out_width = out_ref.shape[1]
    packed_ref[:, :qkv_width] = reordered(qkv_ref[...], halves).astype(BF16)
    packed_ref[:, qkv_width : qkv_width + out_width] = out_ref[...].astype(BF16)
    tail = packed_ref.shape[1] - qkv_width - out_width
    if tail:
        zeros = jnp.zeros((packed_ref.shape[0], tail), BF16)
        packed_ref[:, qkv_width + out_width :] = zeros


def pack_attn(w_qkv, w_out, groups):
    depth = w_qkv.shape[0]
    q_tiles = (groups * PER + 1) // 2
    width = len(tile_halves(groups)) * HD + q_tiles * LANES
    return pl.pallas_call(
        functools.partial(pack_kernel, groups),
        out_shape=like(depth, width),
        in_specs=[IN_VMEM, IN_VMEM],
        out_specs=IN_VMEM,
        compiler_params=vmem(48),
        name="pack_attn",
    )(w_qkv, w_out)


def attn_step_kernel(groups, grad_ref, *refs):
    halves = tile_halves(groups)
    order = [halves.index(i) for i in range(groups * (PER + 2))]
    qkv_width = len(halves) * HD
    qkv_in, out_in, qkv_out, out_out = refs[:3], refs[3:6], refs[6:9], refs[9:]
    of_qkv = reordered(grad_ref[:, :qkv_width].astype(F32), order)
    of_out = grad_ref[:, qkv_width : qkv_width + out_in[0].shape[1]].astype(F32)
    for grad, old, new in ((of_qkv, qkv_in, qkv_out), (of_out, out_in, out_out)):
        stepped = adamw_step(old[0][...], old[1][...], old[2][...], grad, MATRIX_RATE)
        for ref, values in zip(new, stepped):
            ref[...] = values


def attn_step(grads, qkv, out, groups):
    shapes = [like(*v.shape, dtype=F32) for v in qkv + out]
    return pl.pallas_call(
        functools.partial(attn_step_kernel, groups),
        out_shape=shapes,
        in_specs=[IN_VMEM] * 7,
        out_specs=[IN_VMEM] * 6,
        compiler_params=vmem(48),
        name="attn_step",
    )(grads, *qkv, *out)


def exchange(values, bit, count):
    return lax.ppermute(values, "tensor", [(i, i ^ bit) for i in range(count)])


def gather_pieces(own, count):
    first = [exchange(own[0], 1, count), exchange(own[1], 1, count)]
    second = [exchange(own[0], 2, count), exchange(own[1], 2, count)]
    third = [exchange(first[0], 2, count), exchange(second[1], 1, count)]
    pieces = list(own) + first + second + third
    bit = 4
    while bit < count:
        pieces += [exchange(piece, bit, count) for piece in pieces]
        bit *= 2
    return pieces


def gather_whole(own, slots, count):
    return [exchange(own, j, count) for j in slots]


def add(total, *values):
    for value in values:
        total = total + value.astype(F32)
    return total


def fold_shares(shares, count):
    chunk = shares[0].shape[0]
    half = chunk // 2
    while count > 4:
        bit = count // 2
        got = [exchange(v, bit, count) for v in shares[2 * bit - 1 :]]
        own = jnp.concatenate([add(shares[0][:half], got[0]), add(shares[0][half:], got[1])])
        near = [add(a.astype(F32), b).astype(BF16) for a, b in zip(shares[1 : 2 * bit - 1], got[2:])]
        shares = [own] + near
        count = bit
    return shares


def reduce_shares(shares, count, beside=None, near_late=False):
    own, first_0, first_1, second_0, second_1, third_0, third_1 = shares
    half = first_0.shape[0]
    kept = ()
    if beside is not None:
        (third_0, third_1), kept = beside((third_0, third_1))
    far_0 = exchange(third_0, 1, count)
    far_1 = exchange(third_1, 2, count)
    if near_late:
        far_0, far_1, first_0, first_1, second_0, second_1 = tie(
            far_0, far_1, first_0, first_1, second_0, second_1
        )
    got_first_0 = exchange(first_0, 1, count)
    got_second_1 = exchange(second_1, 2, count)
    second_0 = add(second_0.astype(F32), far_0).astype(BF16)
    first_1 = add(first_1.astype(F32), far_1).astype(BF16)
    got_second_0 = exchange(second_0, 2, count)
    got_first_1 = exchange(first_1, 1, count)
    return (
        add(own[:half], got_first_0, got_second_0),
        add(own[half:], got_first_1, got_second_1),
        kept,
    )


def halves_of(values):
    half = values.shape[0] // 2
    return [values[:half], values[half:]]


def norm_back(values, gain, grad):
    scale = lax.rsqrt(jnp.mean(values * values, axis=-1, keepdims=True) + NORM_EPS)
    unscaled = values * scale
    back = grad * gain
    mean = jnp.mean(unscaled * back, axis=-1, keepdims=True)
    return scale * (back - unscaled * mean), jnp.sum(grad * unscaled, axis=0)


def tie(*values):
    return lax.optimization_barrier(values)


def body(
    count,
    dp_count,
    tokens,
    cotangent,
    lengths,
    w_qkv,
    m_qkv,
    v_qkv,
    w_out,
    m_out,
    v_out,
    w_gateup,
    m_gateup,
    v_gateup,
    w_down,
    m_down,
    v_down,
    gains,
    m_gains,
    v_gains,
):
    chunk, model_width = tokens.shape
    row_count = chunk * count
    groups = KV // count
    heads = groups * PER
    mine = lax.axis_index("tensor")
    gain_attn = gains[:model_width]
    gain_ffn = gains[model_width : 2 * model_width]
    gain_query = gains[2 * model_width : 2 * model_width + HD]
    gain_key = gains[2 * model_width + HD :]

    def gather_dp(values):
        return lax.all_gather(values, "dp", axis=0, tiled=True)

    def scatter_dp(values):
        return lax.psum_scatter(values, "dp", scatter_dimension=0, tiled=True)

    inputs = [v.astype(F32) for v in halves_of(tokens)]
    first_local = [norm_rows(v, gain_attn).astype(BF16) for v in inputs]
    first_local, qkv_local, out_local = tie(first_local, w_qkv, w_out.T)
    full_attn = gather_dp(pack_attn(qkv_local, out_local, groups))
    first_pieces = gather_pieces(first_local, count)
    first_pieces[2], first_pieces[5], gateup_local, down_local = tie(
        first_pieces[2], first_pieces[5], w_gateup, w_down
    )
    full_gateup = lax.all_gather(gateup_local.astype(BF16), "dp", axis=1, tiled=True)
    full_down = gather_dp(down_local.T.astype(BF16))

    cotangent, first_pieces = tie(cotangent, first_pieces)
    cot_near = gather_whole(cotangent, (1, 2), count)

    cos, sin = make_tables(lengths, row_count)
    begin_at = layout(lengths[0], row_count)
    scalars = jnp.concatenate([begin_at[::BLK] // BLK, mine[None].astype(jnp.int32)])
    pair_gains = jnp.stack([jnp.tile(gain_query, 2), jnp.tile(gain_key, 2)])
    tables = (cos, sin, pair_gains, begin_at[None, :])

    shares, (attended, mixed, *saved, first_rows) = attend(
        scalars, first_pieces, full_attn, tables, heads, groups, count
    )
    shares, cot_near = tie(shares, cot_near)

    *branch, _ = reduce_shares(fold_shares(shares, count), count)
    middle = [a + b for a, b in zip(inputs, branch)]
    second_local = [norm_rows(v, gain_ffn).astype(BF16) for v in middle]
    second_pieces = gather_pieces(second_local, count)
    cotangent, second_pieces = tie(cotangent, second_pieces)
    cot_pieces = [cotangent] + cot_near + gather_whole(cotangent, range(3, count), count)

    hidden, gate_part, up_part, second_rows = gateup_forward(second_pieces, full_gateup, count)

    grad_down = down_grad(cot_pieces, hidden, count)
    down_sum = scatter_dp(grad_down)
    grad_gate, grad_up = hidden_grad(cot_pieces, full_down, gate_part, up_part, count)
    grad_gateup = gateup_grad(second_rows, grad_gate, grad_up, dp_count)
    grad_gateup, grad_gate, grad_up = tie(grad_gateup, grad_gate, grad_up)
    gateup_sum = scatter_dp(grad_gateup)

    shares = second_shares(range(3, count), grad_gate, grad_up, full_gateup, chunk)
    shares, grad_gate, grad_up = tie(shares, grad_gate, grad_up)
    near = second_shares([1, 2], grad_gate, grad_up, full_gateup, chunk)
    near, grad_gate, grad_up, hidden = tie(near, grad_gate, grad_up, hidden)
    own = second_shares([0], grad_gate, grad_up, full_gateup, chunk)
    *grad_second, _ = reduce_shares(
        fold_shares(own + near + shares, count), count, near_late=True
    )
    feed = down_shares(hidden, full_down, count)
    grad_second, feed = tie(grad_second, feed)

    grad_middle, grad_branch, grad_gain_ffn = [], [], 0.0
    for values, cot, grad in zip(middle, halves_of(cotangent), grad_second):
        back, of_gain = norm_back(values, gain_ffn, grad)
        grad_middle.append(cot.astype(F32) + back)
        grad_branch.append(grad_middle[-1].astype(BF16))
        grad_gain_ffn += of_gain[None, :]

    branch_pieces = gather_pieces(grad_branch, count)
    branch_pieces, feed, down_sum = tie(branch_pieces, feed, down_sum)
    feed = [feed[0]] + [exchange(feed[j], j, count) for j in range(1, count)]

    shares, (grad_mixed, pair_grads, branch_rows) = attend_back(
        scalars, branch_pieces, full_attn, mixed, tables, [attended] + saved, heads, groups, count
    )
    shares, feed[1], feed[2] = tie(shares, feed[1], feed[2])

    def attn_grads(far):
        far, rows = tie(far, first_rows)
        grad_attn, gain_sums = attn_grad(rows, grad_mixed, branch_rows, attended, full_attn)
        gain_grads = pack_gains(gain_sums, gains, grad_gain_ffn, pair_grads)
        return far, tie(grad_attn, gain_grads, gateup_sum, feed)

    *grad_first, (grad_attn, gain_grads, gateup_sum, feed) = reduce_shares(
        fold_shares(shares, count), count, beside=attn_grads
    )
    attn_sum = scatter_dp(grad_attn)
    output = [a + b for a, b in zip(middle, halves_of(add(*feed)))]
    output = jnp.concatenate(output).astype(BF16)
    for axis, size in (("dp", dp_count), ("tensor", count)):
        for i in range(size.bit_length() - 1):
            swap = [(j, j ^ 2**i) for j in range(size)]
            gain_grads += lax.ppermute(gain_grads, axis, swap)

    grad_tokens = jnp.concatenate(
        [
            grad + norm_back(values, gain_attn, back)[0]
            for grad, values, back in zip(grad_middle, inputs, grad_first)
        ]
    )

    turned = lambda values: [v.T for v in values]
    stepped = attn_step(
        attn_sum, [w_qkv, m_qkv, v_qkv], turned([w_out, m_out, v_out]), groups
    )
    gateup_new = adamw_step(w_gateup, m_gateup, v_gateup, gateup_sum[0].astype(F32), MATRIX_RATE)
    down_new = adamw_step(w_down.T, m_down.T, v_down.T, down_sum.astype(F32), MATRIX_RATE)
    gains_new = adamw_step(gains, m_gains, v_gains, gain_grads[0], GAIN_RATE)
    return (
        (output, grad_tokens)
        + tuple(stepped[:3])
        + tuple(turned(stepped[3:]))
        + gateup_new
        + tuple(turned(down_new))
        + gains_new
    )


def solution(mesh):
    rows = P(("dp", "tensor"), None)
    qkv = P("dp", "tensor")
    turned = P("tensor", "dp")
    gateup = P(None, "dp", "tensor")
    weights = (qkv,) * 3 + (turned,) * 3 + (gateup,) * 3 + (turned,) * 3 + (P(),) * 3
    return jax.shard_map(
        functools.partial(body, mesh.shape["tensor"], mesh.shape["dp"]),
        mesh=mesh,
        in_specs=(rows, rows, P("dp", None)) + weights,
        out_specs=(rows, rows) + weights,
        check_vma=False,
    )
```
